512 devices in a mesh: comp: 4 (over z_lo), band: 64 (over x, z_hi, y), cores: 2 (over core).
Axes of the slice: x: 4, y: 8, z: 8 (z_hi: 2, z_lo: 4; z = z_hi * 4 + z_lo), core: 2. Of those that a mesh axis runs over, the one named last changes fastest.
Arguments:
- latent: float32 [2, 4, 128, 240], P(None, None, 'band'), may hold values from -2.5 to 2.5
- section_inputs: bfloat16 [4, 2, 128, 76800], P('comp', None, 'band', 'cores'), may hold values from -6 to 6
- in_weight: float32 [4, 320], P(None, 'cores'), may hold values from -3 to 3
- conv_weight: bfloat16 [4, 921600], P('comp', 'cores'), may hold values from -0.109375 to 0.109375
- out_weight: bfloat16 [320, 4], P('cores'), may hold values from -0.3125 to 0.3125
- timesteps: int32 [4], replicated, may hold values from 0 to 999, as said below
- plan: float32 [1000], replicated, may hold values from 0.04 to 0.95
Outputs:
- denoised: float32 [2, 4, 128, 240], P(None, 'comp', 'band')
- handoff: bfloat16 [4, 2, 128, 76800], P('comp', None, 'band', 'cores')
The draws below stay inside these ranges and needn't reach their ends.
Inputs may be any that keep to these rules, and one draw needn't show every extreme that they name: `timesteps`: falling from step to step, the first entry 999 and the last 0.
All inputs are finite; a program needn't handle non-finite values.
Results may differ from the reference program's by a relative error of at most 0.015.
Values may be sent and summed in bfloat16 or wider, within the bound.
No kernel may reach another device: no remote copies, remote signals or barrier semaphores. Data moves between devices by JAX's collectives and lax.ppermute only.
A program may use at most 64 MiB of HBM per device.

```python
import jax
import jax.numpy as jnp
from jax import lax

CH = 320
LAT = 4
COLS = 240
FRAMES = 2
STEPS = 3
TABLE = 1000
ROWS = 128
COMPS = 4


def draw_timesteps(key, part):
    key = jax.random.fold_in(key, 11)
    step_gap = TABLE // STEPS
    jitter_int = jax.random.randint(key, (STEPS + 1,), 0, step_gap // 2, dtype=jnp.int32)
    position = jnp.arange(STEPS + 1, dtype=jnp.int32)
    middle = (STEPS - position) * step_gap + jitter_int
    first_last = jnp.where(position == 0, TABLE - 1, 0)
    ends = jnp.logical_or(position == 0, position == STEPS)
    return jnp.where(ends, first_last, middle).astype(jnp.int32)


def draw_plan(key, part):
    key = jax.random.fold_in(key, 12)
    position = jnp.arange(TABLE, dtype=jnp.float32) / (TABLE - 1)
    smooth_part = 0.95 * jnp.exp(jnp.log(0.05 / 0.95) * position)
    jitter = jax.random.uniform(key, (TABLE,), jnp.float32, 0.8, 1.0)
    return (smooth_part * jitter).astype(jnp.float32)


def draw_section_inputs(key, part):
    key = jax.random.fold_in(key, 13)
    cell_key, row_key = jax.random.split(key)
    cell_values = jax.random.normal(cell_key, (COMPS, FRAMES, ROWS, CH, COLS), jnp.float32)
    offsets = 0.8 * jax.random.normal(row_key, (COMPS, FRAMES, ROWS, CH, 1), jnp.float32)
    mixed = jnp.clip(cell_values + offsets, -6.0, 6.0)
    return mixed.reshape(COMPS, FRAMES, ROWS, CH * COLS).astype(jnp.bfloat16)


def shard_levels(rng, extent, pieces, low, top_value):
    level, own = 1.0, jax.random.fold_in(rng, 6)
    for dim, parts in pieces:
        heights = jnp.exp(jax.random.uniform(jax.random.fold_in(own, dim), (parts,), jnp.float32, low / len(pieces), top_value / len(pieces)))
        level = level * jnp.repeat(heights, extent[dim] // parts).reshape([-1 if axis == dim else 1 for axis in range(len(extent))])
    return level


def bell_draw(own_key, shape, deviation, bound, cuts=(), held_as=jnp.bfloat16):
    factor_of = shard_levels(own_key, shape, cuts, -0.22, 0.18) if cuts else 1.0
    drawn = jax.random.normal(own_key, shape, jnp.float32) * deviation * factor_of
    return jnp.minimum(jnp.maximum(drawn, -bound), bound).astype(held_as)


def setup_inputs(seed: int = 0) -> dict:
    splits = jax.random.split(jax.random.key(seed), 8)
    return {
        "latent": bell_draw(splits[0], (FRAMES, LAT, ROWS, COLS), 0.25, 2.5, ((2, 64),), jnp.float32),
        "section_inputs": draw_section_inputs(jax.random.fold_in(splits[7], 71), 0),
        "in_weight": bell_draw(splits[2], (LAT, CH), LAT ** -0.5, 3.0, ((1, 2),), jnp.float32),
        "conv_weight": bell_draw(splits[3], (COMPS, 9 * CH * CH), (9 * CH) ** -0.5, 0.109375, ((0, 4), (1, 2))),
        "out_weight": bell_draw(splits[4], (CH, LAT), CH ** -0.5, 0.3125, ((0, 2),)),
        "timesteps": draw_timesteps(jax.random.fold_in(splits[7], 71), 0),
        "plan": draw_plan(jax.random.fold_in(splits[7], 71), 0),
    }


def convolve(flat, weight_flat):
    frames, rows, merged = flat.shape
    acts = flat.reshape(frames, rows, CH, COLS)
    weight = weight_flat.reshape(CH, 3, 3, CH).astype(jnp.float32)
    active = jax.nn.silu(acts.astype(jnp.float32)).astype(jnp.bfloat16)
    padded = jnp.pad(active, ((0, 0), (1, 1), (0, 0), (1, 1)))
    total = jnp.zeros((frames, rows, CH, COLS), jnp.float32)
    for shift_row in range(3):
        for shift_col in range(3):
            window = padded[:, shift_row:shift_row + rows, :, shift_col:shift_col + COLS].astype(jnp.float32)
            total = total + jnp.einsum('friq,oi->froq', window, weight[:, shift_row, shift_col, :], precision=lax.Precision.HIGHEST)
    result = acts.astype(jnp.float32) + total
    return result.astype(jnp.bfloat16).reshape(frames, rows, merged)

def reference(latent, section_inputs, in_weight, conv_weight, out_weight, timesteps, plan):
    state = latent
    cond = section_inputs[0]
    inputs = [section_inputs[c] for c in range(COMPS)]
    outputs = inputs
    for step in range(STEPS):
        proj = jnp.einsum('fjrq,jo->froq', state, in_weight, precision=lax.Precision.HIGHEST)
        proj = proj.reshape(FRAMES, ROWS, CH * COLS)
        inputs[0] = (proj + cond.astype(jnp.float32)).astype(jnp.bfloat16)
        outputs = [convolve(inputs[c], conv_weight[c]) for c in range(COMPS)]
        last = outputs[COMPS - 1].reshape(FRAMES, ROWS, CH, COLS).astype(jnp.float32)
        noise = jnp.einsum('froq,oj->fjrq', last, out_weight.astype(jnp.float32), precision=lax.Precision.HIGHEST)
        alpha_now = plan[timesteps[step]]
        alpha_next = plan[timesteps[step + 1]]
        state = jnp.sqrt(alpha_next / alpha_now) * (state - jnp.sqrt(1.0 - alpha_now) * noise) + jnp.sqrt(1.0 - alpha_next) * noise
        inputs = [inputs[0]] + [outputs[c - 1] for c in range(1, COMPS)]
    return (state, jnp.stack(outputs))
```

```python
import functools

import jax
import jax.numpy as jnp
from jax import lax
from jax.experimental import pallas as pl
from jax.experimental.pallas import tpu as pltpu
from jax.sharding import PartitionSpec as P

STEPS = 3
TAPS = 3
LANES = 128
FRAME = 256
MESSAGE_EXTRA = 16
VMEM_BYTES = 48 * 1024 * 1024


def params():
    return pltpu.CompilerParams(vmem_limit_bytes=VMEM_BYTES)


def in_vmem():
    return pl.BlockSpec(memory_space=pltpu.VMEM)


def weight_kernel(flat_ref, out_ref, held):
    lane = lax.broadcasted_iota(jnp.int32, (80, LANES), 1)
    low = lane < 64

    def rows(start):
        return flat_ref[pl.ds(start, 80, stride=45), :]

    def swapped(value):
        return pltpu.roll(value, 64, axis=1)

    for dq in range(TAPS):
        for parity in range(2):
            tails = []
            for dr in range(TAPS):
                start = 45 * parity + 5 * (3 * dr + dq)
                place, half = start // 2, start % 2
                first, second, third = (rows(place + n) for n in range(3))
                if half:
                    one = swapped(jnp.where(low, second, first))
                    two = swapped(jnp.where(low, third, second))
                    tail_low = False
                else:
                    one, two = first, second
                    tail_low = True
                held[2 * dr, pl.ds(parity, 80, stride=2), :] = one
                held[2 * dr + 1, pl.ds(parity, 80, stride=2), :] = two
                wants_low = dr != 1
                tails.append(third if tail_low == wants_low else swapped(third))
            held[6, pl.ds(parity, 80, stride=2), :] = jnp.where(low, tails[0], tails[1])
            held[7, pl.ds(parity, 80, stride=2), :] = tails[2]
        at = dq * 160
        for tile in range(7):
            out_ref[at : at + 160, tile * LANES : (tile + 1) * LANES] = held[tile].astype(jnp.bfloat16)
        out_ref[at : at + 160, 896:960] = held[7, :, :64].astype(jnp.bfloat16)


def prepare_kernel(core, feat_ref, latent_ref, own_ref, message_ref, state_ref):
    own_ref[...] = jnp.zeros_like(own_ref)
    state_ref[...] = jnp.zeros_like(state_ref)
    for half in range(2):
        for frame in range(2):
            for row in range(2):
                own_ref[row, half * 160 : half * 160 + 160, frame * FRAME : frame * FRAME + 240] = feat_ref[
                    half, frame, row
                ]
    for frame in range(2):
        for row in range(2):
            state_ref[row, 0:4, frame * FRAME : frame * FRAME + 240] = latent_ref[frame, :, row, :]
    me = core()
    message_ref[0:320, :] = own_ref[me]
    state = state_ref[me, 0:4, :]
    high = state.astype(jnp.bfloat16).astype(jnp.float32)
    left = state - high
    middle = left.astype(jnp.bfloat16).astype(jnp.float32)
    low = left - middle
    parts = jnp.concatenate([high, middle, low, jnp.zeros_like(low)], axis=0)
    message_ref[320:336, :] = parts.astype(jnp.bfloat16)


def step_kernel(
    step,
    core,
    plane,
    coef_ref,
    rec_ref,
    edge_ref,
    cond_ref,
    cond_edge_ref,
    state_in_ref,
    in_weight_ref,
    out_weight_ref,
    mine_ref,
    other_ref,
    out_ref,
    state_ref,
    final_ref,
    raw,
    active,
    sums,
    mine,
    other,
    sems,
):
    copies = [
        pltpu.make_async_copy(mine_ref, mine, sems.at[0]),
        pltpu.make_async_copy(other_ref, other, sems.at[1]),
    ]
    for copy in copies:
        copy.start()
    me = core()
    at = plane()
    sources = [
        (1 - me, rec_ref.at[0], cond_ref.at[0]),
        (2 - me, rec_ref.at[1], cond_ref.at[1]),
        (2 * me, edge_ref, cond_edge_ref),
    ]
    lanes = lax.broadcasted_iota(jnp.int32, (1, 2 * FRAME), 1)
    inside = (lanes % FRAME) < 240
    rate, scale_now, scale_next = (coef_ref[0, n] for n in range(3))

    @pl.when(at == 0)
    def _():
        for number, (slot, rec, cond) in enumerate(sources):
            if step == 0:
                if number < 2:
                    state = state_in_ref[number]
                else:
                    extra = edge_ref[320:336, :].astype(jnp.float32)
                    state = (extra[0:4] + extra[4:8]) + extra[8:12]
                    state = jnp.concatenate([state, jnp.zeros_like(state)], axis=0)
            else:
                state = state_in_ref[slot]
                noise = jnp.dot(out_weight_ref[...], rec[0:320, :], preferred_element_type=jnp.float32)[0:8]
                state = rate * (state - scale_now * noise) + scale_next * noise
            state_ref[slot] = state
            for chunk in range(0, 320, 32):
                total = cond[chunk : chunk + 32, :].astype(jnp.float32)
                weight = in_weight_ref[chunk : chunk + 32, :]
                proj = weight[:, 0:1] * state[0:1, :]
                for latent in range(1, 4):
                    proj = proj + weight[:, latent : latent + 1] * state[latent : latent + 1, :]
                raw[slot, chunk : chunk + 32, :] = (proj + total).astype(jnp.bfloat16)

    @pl.when(at != 0)
    def _():
        state_ref[...] = jnp.zeros_like(state_ref)
        for slot, rec, _ in sources:
            raw[slot] = rec[0:320, :]

    for slot in range(3):
        for chunk in range(0, 320, 64):
            value = raw[slot, chunk : chunk + 64, :].astype(jnp.float32)
            value = 0.5 * value * (1.0 + jnp.tanh(0.5 * value))
            place = slot * 256 + chunk if chunk < 256 else 768 + slot * 64
            active[place : place + 64, :] = value.astype(jnp.bfloat16)

    for half, (copy, weight) in enumerate(zip(copies, (mine, other))):
        copy.wait()
        offset = me * 160 if half == 0 else (1 - me) * 160
        sums[...] = jnp.dot(weight[...], active[...], preferred_element_type=jnp.float32)
        for chunk in range(0, 160, 32):
            channels = pl.ds(pl.multiple_of(offset + chunk, 32), 32)
            total = sums[160 + chunk : 160 + chunk + 32, :]
            total = total + pltpu.roll(sums[chunk : chunk + 32, :], 1, axis=1)
            total = total + pltpu.roll(sums[320 + chunk : 320 + chunk + 32, :], 2 * FRAME - 1, axis=1)
            total = total + raw[1, channels, :].astype(jnp.float32)
            out_ref[channels, :] = jnp.where(inside, total, 0.0).astype(jnp.bfloat16)

    if step == STEPS - 1:
        rate, scale_now, scale_next = (coef_ref[1, n] for n in range(3))
        final_ref[...] = rate * state_ref[1]

        @pl.when(at == 3)
        def _():
            noise = jnp.dot(out_weight_ref[...], out_ref[...], preferred_element_type=jnp.float32)[0:8]
            final_ref[...] = (scale_next - rate * scale_now) * noise
    else:
        final_ref[...] = jnp.zeros_like(final_ref)


def prepare(feats, latent):
    core = functools.partial(lax.axis_index, "cores")
    return pl.pallas_call(
        functools.partial(prepare_kernel, core),
        out_shape=[
            jax.ShapeDtypeStruct((2, 320, 2 * FRAME), jnp.bfloat16),
            jax.ShapeDtypeStruct((320 + MESSAGE_EXTRA, 2 * FRAME), jnp.bfloat16),
            jax.ShapeDtypeStruct((2, 8, 2 * FRAME), jnp.float32),
        ],
        in_specs=[in_vmem()] * 2,
        out_specs=[in_vmem()] * 3,
        compiler_params=params(),
        name="prepare",
    )(feats, latent)


def relaid_weight(weight):
    flat = lax.optimization_barrier(weight.astype(jnp.float32)).reshape(-1, LANES)
    return pl.pallas_call(
        weight_kernel,
        out_shape=jax.ShapeDtypeStruct((480, 960), jnp.bfloat16),
        in_specs=[in_vmem()],
        out_specs=in_vmem(),
        scratch_shapes=[pltpu.VMEM((8, 160, LANES), jnp.float32)],
        compiler_params=params(),
        name="relay",
    )(flat)


def run_step(step, coefs, rec, edge, cond, cond_edge, state, in_weight, out_weight, mine, other):
    core = functools.partial(lax.axis_index, "cores")
    plane = functools.partial(lax.axis_index, "comp")
    return pl.pallas_call(
        functools.partial(step_kernel, step, core, plane),
        out_shape=[
            jax.ShapeDtypeStruct((320, 2 * FRAME), jnp.bfloat16),
            jax.ShapeDtypeStruct((3, 8, 2 * FRAME), jnp.float32),
            jax.ShapeDtypeStruct((8, 2 * FRAME), jnp.float32),
        ],
        in_specs=[pl.BlockSpec(memory_space=pltpu.SMEM)] + [in_vmem()] * 7 + [pl.BlockSpec(memory_space=pl.ANY)] * 2,
        out_specs=[in_vmem()] * 3,
        scratch_shapes=[
            pltpu.VMEM((3, 320, 2 * FRAME), jnp.bfloat16),
            pltpu.VMEM((960, 2 * FRAME), jnp.bfloat16),
            pltpu.VMEM((480, 2 * FRAME), jnp.float32),
            pltpu.VMEM((480, 960), jnp.bfloat16),
            pltpu.VMEM((480, 960), jnp.bfloat16),
            pltpu.SemaphoreType.DMA((2,)),
        ],
        compiler_params=params(),
        name=f"step{step}",
    )(coefs, rec, edge, cond, cond_edge, state, in_weight, out_weight, mine, other)


def links(comps, bands):
    def index(comp, band, core):
        return (comp * bands + band) * 2 + core

    edges, diagonals, onward, swap = [], [], [], []
    for comp in range(comps):
        later = (comp + 1) % comps
        for band in range(bands):
            for core in range(2):
                me = index(comp, band, core)
                onward.append((me, index(later, band, core)))
                swap.append((me, index(comp, band, 1 - core)))
                reached = band + 2 * core - 1
                if 0 <= reached < bands:
                    edges.append((me, index(comp, reached, 1 - core)))
                    diagonals.append((me, index(later, reached, 1 - core)))
    return edges, diagonals, onward, swap


def body(latent, section_inputs, in_weight, conv_weight, out_weight, timesteps, plan):
    axes = ("comp", "band", "cores")
    edges, diagonals, onward, swap = links(lax.axis_size("comp"), lax.axis_size("band"))
    plane = lax.axis_index("comp")
    core = lax.axis_index("cores")

    feats = section_inputs[0].reshape(2, 2, 160, 240)
    feats = lax.all_gather(feats, "cores")
    cond, message, state = prepare(feats, latent)
    cond_edge = lax.ppermute(message, axes, edges)

    mine = relaid_weight(conv_weight)
    other = lax.ppermute(mine, axes, swap)
    small = jnp.concatenate([in_weight, out_weight.T.astype(jnp.float32)], axis=0)
    small = lax.all_gather(small, "cores")
    in_columns = jnp.concatenate([small[0, 0:4], small[1, 0:4]], axis=1).T
    in_columns = jnp.pad(in_columns, ((0, 0), (0, 4)))
    out_rows = jnp.concatenate([small[0, 4:8], small[1, 4:8]], axis=1)
    out_rows = jnp.pad(out_rows, ((0, 12), (0, 0))).astype(jnp.bfloat16)

    alphas = plan[timesteps]
    rates = jnp.sqrt(alphas[1:] / alphas[:-1])
    scales = jnp.sqrt(1.0 - alphas)
    coefs = jnp.stack([rates, scales[:-1], scales[1:]], axis=1)

    rec, edge = cond, cond_edge
    for step in range(STEPS):
        pair = coefs[max(step - 1, 0) : max(step - 1, 0) + 2]
        out, state, final = run_step(
            step, pair, rec, edge, cond, cond_edge, state, in_columns, out_rows, mine, other
        )
        if step + 1 < STEPS:
            edge = lax.ppermute(out, axes, diagonals)
            rec = lax.all_gather(lax.ppermute(out, axes, onward), "cores")

    whole = lax.all_gather(out, "cores")
    share = lax.dynamic_slice_in_dim(whole, core * 160, 160, axis=1)
    share = share.reshape(2, 160, 2, FRAME)[..., :240].transpose(2, 0, 1, 3)
    handoff = share.reshape(1, 2, 2, 160 * 240)

    total = lax.psum(final[0:4], "comp")
    total = lax.all_gather(lax.dynamic_slice_in_dim(total, plane, 1, axis=0)[0], "cores")
    denoised = total.reshape(2, 2, FRAME)[..., :240].transpose(1, 0, 2)[:, None]
    return denoised, handoff


def solution(mesh):
    in_specs = (
        P(None, None, "band", None),
        P("comp", None, "band", "cores"),
        P(None, "cores"),
        P("comp", "cores"),
        P("cores", None),
        P(),
        P(),
    )
    out_specs = (P(None, "comp", "band", None), P("comp", None, "band", "cores"))
    return jax.shard_map(body, mesh=mesh, in_specs=in_specs, out_specs=out_specs, check_vma=False)
```

```python
import functools

import jax
import jax.numpy as jnp
from jax import lax
from jax.experimental import pallas as pl
from jax.experimental.pallas import tpu as pltpu
from jax.sharding import PartitionSpec as P

STEPS = 3
TAPS = 3
LANES = 128
FRAME = 256
MESSAGE_EXTRA = 16
VMEM_BYTES = 48 * 1024 * 1024


def params():
    return pltpu.CompilerParams(vmem_limit_bytes=VMEM_BYTES)


def in_vmem():
    return pl.BlockSpec(memory_space=pltpu.VMEM)


def weight_kernel(flat_ref, out_ref, held):
    lane = lax.broadcasted_iota(jnp.int32, (80, LANES), 1)
    low = lane < 64

    def rows(start):
        return flat_ref[pl.ds(start, 80, stride=45), :]

    def swapped(value):
        return pltpu.roll(value, 64, axis=1)

    for dq in range(TAPS):
        for parity in range(2):
            tails = []
            for dr in range(TAPS):
                start = 45 * parity + 5 * (3 * dr + dq)
                place, half = start // 2, start % 2
                first, second, third = (rows(place + n) for n in range(3))
                if half:
                    one = swapped(jnp.where(low, second, first))
                    two = swapped(jnp.where(low, third, second))
                    tail_low = False
                else:
                    one, two = first, second
                    tail_low = True
                held[2 * dr, pl.ds(parity, 80, stride=2), :] = one
                held[2 * dr + 1, pl.ds(parity, 80, stride=2), :] = two
                wants_low = dr != 1
                tails.append(third if tail_low == wants_low else swapped(third))
            held[6, pl.ds(parity, 80, stride=2), :] = jnp.where(low, tails[0], tails[1])
            held[7, pl.ds(parity, 80, stride=2), :] = tails[2]
        at = dq * 160
        for tile in range(7):
            out_ref[at : at + 160, tile * LANES : (tile + 1) * LANES] = held[tile].astype(jnp.bfloat16)
        out_ref[at : at + 160, 896:960] = held[7, :, :64].astype(jnp.bfloat16)


def prepare_kernel(core, feat_ref, latent_ref, own_ref, message_ref, state_ref):
    own_ref[...] = jnp.zeros_like(own_ref)
    state_ref[...] = jnp.zeros_like(state_ref)
    for half in range(2):
        for frame in range(2):
            for row in range(2):
                own_ref[row, half * 160 : half * 160 + 160, frame * FRAME : frame * FRAME + 240] = feat_ref[
                    half, frame, row
                ]
    for frame in range(2):
        for row in range(2):
            state_ref[row, 0:4, frame * FRAME : frame * FRAME + 240] = latent_ref[frame, :, row, :]
    me = core()
    message_ref[0:320, :] = own_ref[me]
    state = state_ref[me, 0:4, :]
    high = state.astype(jnp.bfloat16).astype(jnp.float32)
    left = state - high
    middle = left.astype(jnp.bfloat16).astype(jnp.float32)
    low = left - middle
    parts = jnp.concatenate([high, middle, low, jnp.zeros_like(low)], axis=0)
    message_ref[320:336, :] = parts.astype(jnp.bfloat16)


def step_kernel(
    step,
    core,
    plane,
    coef_ref,
    rec_ref,
    edge_ref,
    cond_ref,
    cond_edge_ref,
    noise_ref,
    noise_edge_ref,
    state_in_ref,
    in_weight_ref,
    out_weight_ref,
    mine_ref,
    other_ref,
    out_ref,
    state_ref,
    final_ref,
    raw,
    active,
    sums,
):
    me = core()
    at = plane()
    sources = [
        (1 - me, rec_ref.at[0], cond_ref.at[0], noise_ref.at[0]),
        (2 - me, rec_ref.at[1], cond_ref.at[1], noise_ref.at[1]),
        (2 * me, edge_ref, cond_edge_ref, noise_edge_ref),
    ]
    lanes = lax.broadcasted_iota(jnp.int32, (1, 2 * FRAME), 1)
    inside = (lanes % FRAME) < 240
    rate, scale_now, scale_next = (coef_ref[0, n] for n in range(3))

    @pl.when(at == 0)
    def _():
        for number, (slot, _, cond, noise_row) in enumerate(sources):
            if step == 0:
                if number < 2:
                    state = state_in_ref[number]
                else:
                    extra = cond_edge_ref[320:336, :].astype(jnp.float32)
                    state = (extra[0:4] + extra[4:8]) + extra[8:12]
                    state = jnp.concatenate([state, jnp.zeros_like(state)], axis=0)
            else:
                state = state_in_ref[slot]
                noise = noise_row[...]
                state = rate * (state - scale_now * noise) + scale_next * noise
            state_ref[slot] = state
            for chunk in range(0, 320, 32):
                total = cond[chunk : chunk + 32, :].astype(jnp.float32)
                weight = in_weight_ref[chunk : chunk + 32, :]
                proj = weight[:, 0:1] * state[0:1, :]
                for latent in range(1, 4):
                    proj = proj + weight[:, latent : latent + 1] * state[latent : latent + 1, :]
                raw[slot, chunk : chunk + 32, :] = (proj + total).astype(jnp.bfloat16)

    @pl.when(at != 0)
    def _():
        state_ref[...] = jnp.zeros_like(state_ref)
        for slot, rec, _, _ in sources:
            raw[slot] = rec[0:320, :]

    for slot in range(3):
        for chunk in range(0, 320, 64):
            value = raw[slot, chunk : chunk + 64, :].astype(jnp.float32)
            value = 0.5 * value * (1.0 + jnp.tanh(0.5 * value))
            place = slot * 256 + chunk if chunk < 256 else 768 + slot * 64
            active[place : place + 64, :] = value.astype(jnp.bfloat16)

    for half, weight in enumerate((mine_ref, other_ref)):
        offset = me * 160 if half == 0 else (1 - me) * 160
        sums[...] = jnp.dot(weight[...], active[...], preferred_element_type=jnp.float32)
        for chunk in range(0, 160, 32):
            channels = pl.ds(pl.multiple_of(offset + chunk, 32), 32)
            total = sums[160 + chunk : 160 + chunk + 32, :]
            total = total + pltpu.roll(sums[chunk : chunk + 32, :], 1, axis=1)
            total = total + pltpu.roll(sums[320 + chunk : 320 + chunk + 32, :], 2 * FRAME - 1, axis=1)
            total = total + raw[1, channels, :].astype(jnp.float32)
            out_ref[channels, :] = jnp.where(inside, total, 0.0).astype(jnp.bfloat16)

    final_ref[...] = jnp.zeros_like(final_ref)

    @pl.when(at == 3)
    def _():
        noise = jnp.dot(out_weight_ref[...], out_ref[...], preferred_element_type=jnp.float32)[0:8]
        if step == STEPS - 1:
            noise = (coef_ref[1, 2] - coef_ref[1, 0] * coef_ref[1, 1]) * noise
        final_ref[...] = noise

    if step == STEPS - 1:

        @pl.when(at == 0)
        def _():
            final_ref[...] = coef_ref[1, 0] * state_ref[1]


def prepare(feats, latent):
    core = functools.partial(lax.axis_index, "cores")
    return pl.pallas_call(
        functools.partial(prepare_kernel, core),
        out_shape=[
            jax.ShapeDtypeStruct((2, 320, 2 * FRAME), jnp.bfloat16),
            jax.ShapeDtypeStruct((320 + MESSAGE_EXTRA, 2 * FRAME), jnp.bfloat16),
            jax.ShapeDtypeStruct((2, 8, 2 * FRAME), jnp.float32),
        ],
        in_specs=[in_vmem()] * 2,
        out_specs=[in_vmem()] * 3,
        compiler_params=params(),
        name="prepare",
    )(feats, latent)


def relaid_weight(weight):
    flat = lax.optimization_barrier(weight.astype(jnp.float32)).reshape(-1, LANES)
    return pl.pallas_call(
        weight_kernel,
        out_shape=jax.ShapeDtypeStruct((480, 960), jnp.bfloat16),
        in_specs=[in_vmem()],
        out_specs=in_vmem(),
        scratch_shapes=[pltpu.VMEM((8, 160, LANES), jnp.float32)],
        compiler_params=params(),
        name="relay",
    )(flat)


def run_step(step, coefs, rec, edge, cond, cond_edge, noise, noise_edge, state, in_weight, out_weight, mine, other):
    core = functools.partial(lax.axis_index, "cores")
    plane = functools.partial(lax.axis_index, "comp")
    return pl.pallas_call(
        functools.partial(step_kernel, step, core, plane),
        out_shape=[
            jax.ShapeDtypeStruct((320, 2 * FRAME), jnp.bfloat16),
            jax.ShapeDtypeStruct((3, 8, 2 * FRAME), jnp.float32),
            jax.ShapeDtypeStruct((8, 2 * FRAME), jnp.float32),
        ],
        in_specs=[pl.BlockSpec(memory_space=pltpu.SMEM)] + [in_vmem()] * 11,
        out_specs=[in_vmem()] * 3,
        scratch_shapes=[
            pltpu.VMEM((3, 320, 2 * FRAME), jnp.bfloat16),
            pltpu.VMEM((960, 2 * FRAME), jnp.bfloat16),
            pltpu.VMEM((480, 2 * FRAME), jnp.float32),
        ],
        compiler_params=params(),
        name=f"step{step}",
    )(coefs, rec, edge, cond, cond_edge, noise, noise_edge, state, in_weight, out_weight, mine, other)


def links(comps, bands):
    def index(comp, band, core):
        return (comp * bands + band) * 2 + core

    edges, swap = [], []
    onward, diagonals = [], []
    noise_onward, noise_diagonals = [], []
    for comp in range(comps):
        last = comp == comps - 1
        later = 0 if last else comp + 1
        for band in range(bands):
            for core in range(2):
                me = index(comp, band, core)
                (noise_onward if last else onward).append((me, index(later, band, core)))
                swap.append((me, index(comp, band, 1 - core)))
                reached = band + 2 * core - 1
                if 0 <= reached < bands:
                    edges.append((me, index(comp, reached, 1 - core)))
                    pair = (me, index(later, reached, 1 - core))
                    (noise_diagonals if last else diagonals).append(pair)
    return edges, swap, onward, diagonals, noise_onward, noise_diagonals


def body(latent, section_inputs, in_weight, conv_weight, out_weight, timesteps, plan):
    axes = ("comp", "band", "cores")
    edges, swap, onward, diagonals, noise_onward, noise_diagonals = links(
        lax.axis_size("comp"), lax.axis_size("band")
    )
    plane = lax.axis_index("comp")
    core = lax.axis_index("cores")

    feats = section_inputs[0].reshape(2, 2, 160, 240)
    feats = lax.all_gather(feats, "cores")
    cond, message, state = prepare(feats, latent)
    cond_edge = lax.ppermute(message, axes, edges)

    mine = relaid_weight(conv_weight)
    other = lax.ppermute(mine, axes, swap)
    small = jnp.concatenate([in_weight, out_weight.T.astype(jnp.float32)], axis=0)
    small = lax.all_gather(small, "cores")
    in_columns = jnp.concatenate([small[0, 0:4], small[1, 0:4]], axis=1).T
    in_columns = jnp.pad(in_columns, ((0, 0), (0, 4)))
    out_rows = jnp.concatenate([small[0, 4:8], small[1, 4:8]], axis=1)
    out_rows = jnp.pad(out_rows, ((0, 12), (0, 0))).astype(jnp.bfloat16)

    alphas = plan[timesteps]
    rates = jnp.sqrt(alphas[1:] / alphas[:-1])
    scales = jnp.sqrt(1.0 - alphas)
    coefs = jnp.stack([rates, scales[:-1], scales[1:]], axis=1)

    rec, edge = cond, cond_edge
    noise_edge = jnp.zeros((8, 2 * FRAME), jnp.float32)
    noise = jnp.zeros((2, 8, 2 * FRAME), jnp.float32)
    for step in range(STEPS):
        pair = coefs[max(step - 1, 0) : max(step - 1, 0) + 2]
        out, state, final = run_step(
            step, pair, rec, edge, cond, cond_edge, noise, noise_edge, state, in_columns, out_rows, mine, other
        )
        if step + 1 < STEPS:
            rec = lax.ppermute(out, axes, onward)
            edge = lax.ppermute(out, axes, diagonals)
            noise = lax.ppermute(final, axes, noise_onward)
            noise_edge = lax.ppermute(final, axes, noise_diagonals)
            noise = lax.all_gather(noise, "cores")
            rec = lax.all_gather(rec, "cores")

    whole = lax.all_gather(out, "cores")
    share = lax.dynamic_slice_in_dim(whole, core * 160, 160, axis=1)
    share = share.reshape(2, 160, 2, FRAME)[..., :240].transpose(2, 0, 1, 3)
    handoff = share.reshape(1, 2, 2, 160 * 240)

    total = lax.psum(final[0:4], "comp")
    total = lax.all_gather(lax.dynamic_slice_in_dim(total, plane, 1, axis=0)[0], "cores")
    denoised = total.reshape(2, 2, FRAME)[..., :240].transpose(1, 0, 2)[:, None]
    return denoised, handoff


def solution(mesh):
    in_specs = (
        P(None, None, "band", None),
        P("comp", None, "band", "cores"),
        P(None, "cores"),
        P("comp", "cores"),
        P("cores", None),
        P(),
        P(),
    )
    out_specs = (P(None, "comp", "band", None), P("comp", None, "band", "cores"))
    return jax.shard_map(body, mesh=mesh, in_specs=in_specs, out_specs=out_specs, check_vma=False)
```

```python
import functools

import jax
import jax.numpy as jnp
from jax import lax
from jax.experimental import pallas as pl
from jax.experimental.pallas import tpu as pltpu
from jax.sharding import PartitionSpec as P

STEPS = 3
TAPS = 3
LANES = 128
FRAME = 256
MESSAGE_EXTRA = 16
VMEM_BYTES = 14 * 1024 * 1024


def params():
    return pltpu.CompilerParams(vmem_limit_bytes=VMEM_BYTES)


def in_vmem():
    return pl.BlockSpec(memory_space=pltpu.VMEM)


def weight_kernel(flat_ref, out_ref, held):
    lane = lax.broadcasted_iota(jnp.int32, (80, LANES), 1)
    low = lane < 64

    def rows(start):
        return flat_ref[pl.ds(start, 80, stride=45), :]

    def swapped(value):
        return pltpu.roll(value, 64, axis=1)

    for dq in range(TAPS):
        for parity in range(2):
            tails = []
            for dr in range(TAPS):
                start = 45 * parity + 5 * (3 * dr + dq)
                place, half = start // 2, start % 2
                first, second, third = (rows(place + n) for n in range(3))
                if half:
                    one = swapped(jnp.where(low, second, first))
                    two = swapped(jnp.where(low, third, second))
                    tail_low = False
                else:
                    one, two = first, second
                    tail_low = True
                held[2 * dr, pl.ds(parity, 80, stride=2), :] = one
                held[2 * dr + 1, pl.ds(parity, 80, stride=2), :] = two
                wants_low = dr != 1
                tails.append(third if tail_low == wants_low else swapped(third))
            held[6, pl.ds(parity, 80, stride=2), :] = jnp.where(low, tails[0], tails[1])
            held[7, pl.ds(parity, 80, stride=2), :] = tails[2]
        at = dq * 160
        for tile in range(7):
            out_ref[at : at + 160, tile * LANES : (tile + 1) * LANES] = held[tile].astype(jnp.bfloat16)
        out_ref[at : at + 160, 896:960] = held[7, :, :64].astype(jnp.bfloat16)


def prepare_kernel(core, feat_ref, latent_ref, own_ref, message_ref, state_ref, latent, sem):
    copy = pltpu.make_async_copy(latent_ref, latent, sem)
    copy.start()
    own_ref[...] = jnp.zeros_like(own_ref)
    state_ref[...] = jnp.zeros_like(state_ref)
    for half in range(2):
        for frame in range(2):
            for row in range(2):
                own_ref[row, half * 160 : half * 160 + 160, frame * FRAME : frame * FRAME + 240] = feat_ref[
                    half, frame, row
                ]
    me = core()
    message_ref[0:320, :] = own_ref[me]
    copy.wait()
    for frame in range(2):
        for row in range(2):
            state_ref[row, 0:4, frame * FRAME : frame * FRAME + 240] = latent[frame, :, row, :]
    state = state_ref[me, 0:4, :]
    high = state.astype(jnp.bfloat16).astype(jnp.float32)
    left = state - high
    middle = left.astype(jnp.bfloat16).astype(jnp.float32)
    low = left - middle
    parts = jnp.concatenate([high, middle, low, jnp.zeros_like(low)], axis=0)
    message_ref[320:336, :] = parts.astype(jnp.bfloat16)


def swish(value):
    value = value.astype(jnp.float32)
    return (0.5 * value * (1.0 + jnp.tanh(0.5 * value))).astype(jnp.bfloat16)


def project(slot, state, cond, in_weight_ref, raw):
    for chunk in range(0, 320, 32):
        total = cond[chunk : chunk + 32, :].astype(jnp.float32)
        weight = in_weight_ref[chunk : chunk + 32, :]
        proj = weight[:, 0:1] * state[0:1, :]
        for latent in range(1, 4):
            proj = proj + weight[:, latent : latent + 1] * state[latent : latent + 1, :]
        raw[slot, chunk : chunk + 32, :] = (proj + total).astype(jnp.bfloat16)


def latent_kernel(
    core, plane, coef_ref, noise_ref, noise_edge_ref, state_in_ref, in_weight_ref, cond_ref, cond_edge_ref, input_ref, state_ref
):
    me = core()
    at = plane()

    @pl.when(at == 0)
    def _():
        rate, scale_now, scale_next = (coef_ref[0, n] for n in range(3))
        for slot, noise_row, cond in (
            (1 - me, noise_ref.at[0], cond_ref.at[0]),
            (2 - me, noise_ref.at[1], cond_ref.at[1]),
            (2 * me, noise_edge_ref, cond_edge_ref),
        ):
            noise = noise_row[...]
            state = state_in_ref[slot]
            state = rate * (state - scale_now * noise) + scale_next * noise
            state_ref[slot] = state
            project(slot, state, cond, in_weight_ref, input_ref)

    @pl.when(at != 0)
    def _():
        state_ref[...] = jnp.zeros_like(state_ref)


def edge_kernel(edge_ref, out_ref):
    for chunk in range(0, 320, 64):
        out_ref[chunk : chunk + 64, :] = swish(edge_ref[chunk : chunk + 64, :])


def step_kernel(
    step,
    core,
    plane,
    coef_ref,
    input_ref,
    state_in_ref,
    edge_ref,
    rec_ref,
    in_weight_ref,
    out_weight_ref,
    mine_ref,
    other_ref,
    out_ref,
    state_ref,
    final_ref,
    raw,
    active,
    sums,
):
    me = core()
    at = plane()
    lanes = lax.broadcasted_iota(jnp.int32, (1, 2 * FRAME), 1)
    inside = (lanes % FRAME) < 240

    def activate(slot, rows):
        start = pl.multiple_of(slot * 256, 256)
        tail = pl.multiple_of(768 + slot * 64, 64)
        for chunk in range(0, 320, 64):
            place = start + chunk if chunk < 256 else tail
            active[pl.ds(place, 64), :] = rows(chunk)

    @pl.when(at == 0)
    def _():
        if step == 0:
            extra = edge_ref[320:336, :].astype(jnp.float32)
            halo = (extra[0:4] + extra[4:8]) + extra[8:12]
            halo = jnp.concatenate([halo, jnp.zeros_like(halo)], axis=0)
            for slot, state, cond in (
                (1 - me, state_in_ref[0], rec_ref.at[0]),
                (2 - me, state_in_ref[1], rec_ref.at[1]),
                (2 * me, halo, edge_ref),
            ):
                state_ref[slot] = state
                project(slot, state, cond, in_weight_ref, raw)
        else:
            state_ref[...] = state_in_ref[...]
            raw[...] = input_ref[...]
        for slot in range(3):
            activate(slot, lambda chunk, slot=slot: swish(raw[slot, chunk : chunk + 64, :]))

    @pl.when(at != 0)
    def _():
        state_ref[...] = jnp.zeros_like(state_ref)
        raw[1] = rec_ref[me]
        for row in range(2):
            activate(row + 1 - me, lambda chunk, row=row: swish(rec_ref[row, chunk : chunk + 64, :]))
        activate(2 * me, lambda chunk: swish(edge_ref[chunk : chunk + 64, :]))

    for half, weight in enumerate((mine_ref, other_ref)):
        offset = me * 160 if half == 0 else (1 - me) * 160
        sums[...] = jnp.dot(weight[...], active[...], preferred_element_type=jnp.float32)
        for chunk in range(0, 160, 32):
            channels = pl.ds(pl.multiple_of(offset + chunk, 32), 32)
            total = sums[160 + chunk : 160 + chunk + 32, :]
            total = total + pltpu.roll(sums[chunk : chunk + 32, :], 1, axis=1)
            total = total + pltpu.roll(sums[320 + chunk : 320 + chunk + 32, :], 2 * FRAME - 1, axis=1)
            total = total + raw[1, channels, :].astype(jnp.float32)
            out_ref[channels, :] = jnp.where(inside, total, 0.0).astype(jnp.bfloat16)

    final_ref[...] = jnp.zeros_like(final_ref)

    @pl.when(at == 3)
    def _():
        noise = jnp.dot(out_weight_ref[...], out_ref[...], preferred_element_type=jnp.float32)[0:8]
        if step == STEPS - 1:
            noise = (coef_ref[1, 2] - coef_ref[1, 0] * coef_ref[1, 1]) * noise
        final_ref[...] = noise

    if step == STEPS - 1:

        @pl.when(at == 0)
        def _():
            final_ref[...] = coef_ref[1, 0] * state_ref[1]


def prepare(feats, latent):
    core = functools.partial(lax.axis_index, "cores")
    return pl.pallas_call(
        functools.partial(prepare_kernel, core),
        out_shape=[
            jax.ShapeDtypeStruct((2, 320, 2 * FRAME), jnp.bfloat16),
            jax.ShapeDtypeStruct((320 + MESSAGE_EXTRA, 2 * FRAME), jnp.bfloat16),
            jax.ShapeDtypeStruct((2, 8, 2 * FRAME), jnp.float32),
        ],
        in_specs=[in_vmem(), pl.BlockSpec(memory_space=pl.ANY)],
        out_specs=[in_vmem()] * 3,
        scratch_shapes=[pltpu.VMEM(latent.shape, latent.dtype), pltpu.SemaphoreType.DMA],
        compiler_params=params(),
        name="prepare",
    )(feats, latent)


def relaid_weight(weight):
    flat = lax.optimization_barrier(weight.astype(jnp.float32)).reshape(-1, LANES)
    return pl.pallas_call(
        weight_kernel,
        out_shape=jax.ShapeDtypeStruct((480, 960), jnp.bfloat16),
        in_specs=[in_vmem()],
        out_specs=in_vmem(),
        scratch_shapes=[pltpu.VMEM((8, 160, LANES), jnp.float32)],
        compiler_params=params(),
        name="relay",
    )(flat)


def hint(micros):
    return pl.CostEstimate(flops=int(micros * 1e9), bytes_accessed=0, transcendentals=0)


def run_latent(coefs, noise, noise_edge, state, in_weight, cond, cond_edge):
    core = functools.partial(lax.axis_index, "cores")
    plane = functools.partial(lax.axis_index, "comp")
    return pl.pallas_call(
        functools.partial(latent_kernel, core, plane),
        out_shape=[
            jax.ShapeDtypeStruct((3, 320, 2 * FRAME), jnp.bfloat16),
            jax.ShapeDtypeStruct((3, 8, 2 * FRAME), jnp.float32),
        ],
        in_specs=[pl.BlockSpec(memory_space=pltpu.SMEM)] + [in_vmem()] * 6,
        out_specs=[in_vmem()] * 2,
        compiler_params=params(),
        cost_estimate=hint(3),
        name="latent",
    )(coefs, noise, noise_edge, state, in_weight, cond, cond_edge)


def run_edge(edge):
    return pl.pallas_call(
        edge_kernel,
        out_shape=jax.ShapeDtypeStruct((320, 2 * FRAME), jnp.bfloat16),
        in_specs=[in_vmem()],
        out_specs=in_vmem(),
        compiler_params=params(),
        cost_estimate=hint(20),
        name="edge",
    )(edge)


def run_step(step, coefs, rec, edge, inputs, state, in_weight, out_weight, mine, other):
    core = functools.partial(lax.axis_index, "cores")
    plane = functools.partial(lax.axis_index, "comp")
    return pl.pallas_call(
        functools.partial(step_kernel, step, core, plane),
        out_shape=[
            jax.ShapeDtypeStruct((320, 2 * FRAME), jnp.bfloat16),
            jax.ShapeDtypeStruct((3, 8, 2 * FRAME), jnp.float32),
            jax.ShapeDtypeStruct((8, 2 * FRAME), jnp.float32),
        ],
        in_specs=[pl.BlockSpec(memory_space=pltpu.SMEM)] + [in_vmem()] * 8,
        out_specs=[in_vmem()] * 3,
        scratch_shapes=[
            pltpu.VMEM((3, 320, 2 * FRAME), jnp.bfloat16),
            pltpu.VMEM((960, 2 * FRAME), jnp.bfloat16),
            pltpu.VMEM((480, 2 * FRAME), jnp.float32),
        ],
        compiler_params=params(),
        name=f"step{step}",
    )(coefs, inputs, state, edge, rec, in_weight, out_weight, mine, other)


def copy_kernel(in_ref, out_ref):
    out_ref[...] = in_ref[...]


def copied(row):
    return pl.pallas_call(
        copy_kernel,
        out_shape=jax.ShapeDtypeStruct(row.shape, row.dtype),
        in_specs=[in_vmem()],
        out_specs=in_vmem(),
        compiler_params=params(),
        cost_estimate=hint(20),
        name="copy_row",
    )(row)


def links(comps, bands):
    def index(comp, band, core):
        return (comp * bands + band) * 2 + core

    edges, swap = [], []
    onward, diagonals = [], []
    noise_onward, noise_diagonals = [], []
    for comp in range(comps):
        last = comp == comps - 1
        later = 0 if last else comp + 1
        for band in range(bands):
            for core in range(2):
                me = index(comp, band, core)
                (noise_onward if last else onward).append((me, index(later, band, core)))
                swap.append((me, index(comp, band, 1 - core)))
                reached = band + 2 * core - 1
                if 0 <= reached < bands:
                    edges.append((me, index(comp, reached, 1 - core)))
                    pair = (me, index(later, reached, 1 - core))
                    (noise_diagonals if last else diagonals).append(pair)
    return edges, swap, onward, diagonals, noise_onward, noise_diagonals


def body(latent, section_inputs, in_weight, conv_weight, out_weight, timesteps, plan):
    axes = ("comp", "band", "cores")
    edges, swap, onward, diagonals, noise_onward, noise_diagonals = links(
        lax.axis_size("comp"), lax.axis_size("band")
    )
    plane = lax.axis_index("comp")
    core = lax.axis_index("cores")

    feats = section_inputs[0].reshape(2, 2, 160, 240)
    feats = lax.all_gather(feats, "cores")
    cond, message, state = prepare(feats, latent)
    conv_weight, message = lax.optimization_barrier((conv_weight, message))
    cond_edge = lax.ppermute(message, axes, edges)

    mine = relaid_weight(conv_weight)
    other = lax.ppermute(mine, axes, swap)
    small = jnp.concatenate([in_weight, out_weight.T.astype(jnp.float32)], axis=0)
    small = lax.all_gather(small, "cores")
    in_columns = jnp.concatenate([small[0, 0:4], small[1, 0:4]], axis=1).T
    in_columns = jnp.pad(in_columns, ((0, 0), (0, 4)))
    out_rows = jnp.concatenate([small[0, 4:8], small[1, 4:8]], axis=1)
    out_rows = jnp.pad(out_rows, ((0, 12), (0, 0))).astype(jnp.bfloat16)

    alphas = plan[timesteps]
    rates = jnp.sqrt(alphas[1:] / alphas[:-1])
    scales = jnp.sqrt(1.0 - alphas)
    coefs = jnp.stack([rates, scales[:-1], scales[1:]], axis=1)

    rec, edge = cond, cond_edge
    inputs = jnp.zeros((3, 16, LANES), jnp.bfloat16)
    for step in range(STEPS):
        pair = coefs[max(step - 1, 0) : max(step - 1, 0) + 2]
        out, state, final = run_step(step, pair, rec, edge, inputs, state, in_columns, out_rows, mine, other)
        if step + 1 < STEPS:
            edge = lax.ppermute(out, axes, diagonals)
            rec = lax.ppermute(out, axes, onward)
            rec = lax.all_gather(rec, "cores")
            noise = lax.all_gather(lax.ppermute(final, axes, noise_onward), "cores")
            noise_edge = lax.ppermute(final, axes, noise_diagonals)
            state = copied(state)
            inputs, state = run_latent(
                coefs[step : step + 2], noise, noise_edge, state, in_columns, cond, cond_edge
            )

    whole = lax.all_gather(out, "cores")
    share = lax.dynamic_slice_in_dim(whole, core * 160, 160, axis=1)
    share = share.reshape(2, 160, 2, FRAME)[..., :240].transpose(2, 0, 1, 3)
    handoff = share.reshape(1, 2, 2, 160 * 240)

    total = lax.psum(final[0:4], "comp")
    total = lax.all_gather(lax.dynamic_slice_in_dim(total, plane, 1, axis=0)[0], "cores")
    denoised = total.reshape(2, 2, FRAME)[..., :240].transpose(1, 0, 2)[:, None]
    return denoised, handoff


def solution(mesh):
    in_specs = (
        P(None, None, "band", None),
        P("comp", None, "band", "cores"),
        P(None, "cores"),
        P("comp", "cores"),
        P("cores", None),
        P(),
        P(),
    )
    out_specs = (P(None, "comp", "band", None), P("comp", None, "band", "cores"))
    return jax.shard_map(body, mesh=mesh, in_specs=in_specs, out_specs=out_specs, check_vma=False)
```

```python
import functools

import jax
import jax.numpy as jnp
from jax import lax
from jax.experimental import pallas as pl
from jax.experimental.pallas import tpu as pltpu
from jax.sharding import PartitionSpec as P

STEPS = 3
TAPS = 3
LANES = 128
FRAME = 256
MESSAGE_EXTRA = 16
VMEM_BYTES = 14 * 1024 * 1024


def params():
    return pltpu.CompilerParams(vmem_limit_bytes=VMEM_BYTES)


def in_vmem():
    return pl.BlockSpec(memory_space=pltpu.VMEM)


def weight_kernel(flat_ref, out_ref, held):
    lane = lax.broadcasted_iota(jnp.int32, (80, LANES), 1)
    low = lane < 64

    def rows(start):
        return flat_ref[pl.ds(start, 80, stride=45), :]

    def swapped(value):
        return pltpu.roll(value, 64, axis=1)

    for dq in range(TAPS):
        for parity in range(2):
            tails = []
            for dr in range(TAPS):
                start = 45 * parity + 5 * (3 * dr + dq)
                place, half = start // 2, start % 2
                first, second, third = (rows(place + n) for n in range(3))
                if half:
                    one = swapped(jnp.where(low, second, first))
                    two = swapped(jnp.where(low, third, second))
                    tail_low = False
                else:
                    one, two = first, second
                    tail_low = True
                held[2 * dr, pl.ds(parity, 80, stride=2), :] = one
                held[2 * dr + 1, pl.ds(parity, 80, stride=2), :] = two
                wants_low = dr != 1
                tails.append(third if tail_low == wants_low else swapped(third))
            held[6, pl.ds(parity, 80, stride=2), :] = jnp.where(low, tails[0], tails[1])
            held[7, pl.ds(parity, 80, stride=2), :] = tails[2]
        at = dq * 160
        for tile in range(7):
            out_ref[at : at + 160, tile * LANES : (tile + 1) * LANES] = held[tile].astype(jnp.bfloat16)
        out_ref[at : at + 160, 896:960] = held[7, :, :64].astype(jnp.bfloat16)


def prepare_kernel(core, feat_ref, latent_ref, own_ref, message_ref, state_ref, latent, sem):
    copy = pltpu.make_async_copy(latent_ref, latent, sem)
    copy.start()
    own_ref[...] = jnp.zeros_like(own_ref)
    state_ref[...] = jnp.zeros_like(state_ref)
    for half in range(2):
        for frame in range(2):
            for row in range(2):
                own_ref[row, half * 160 : half * 160 + 160, frame * FRAME : frame * FRAME + 240] = feat_ref[
                    half, frame, row
                ]
    me = core()
    message_ref[0:320, :] = own_ref[me]
    copy.wait()
    for frame in range(2):
        for row in range(2):
            state_ref[row, 0:4, frame * FRAME : frame * FRAME + 240] = latent[frame, :, row, :]
    state = state_ref[me, 0:4, :]
    high = state.astype(jnp.bfloat16).astype(jnp.float32)
    left = state - high
    middle = left.astype(jnp.bfloat16).astype(jnp.float32)
    low = left - middle
    parts = jnp.concatenate([high, middle, low, jnp.zeros_like(low)], axis=0)
    message_ref[320:336, :] = parts.astype(jnp.bfloat16)


def swish(value):
    value = value.astype(jnp.float32)
    return (0.5 * value * (1.0 + jnp.tanh(0.5 * value))).astype(jnp.bfloat16)


def project(slot, state, cond, in_weight_ref, raw):
    for chunk in range(0, 320, 32):
        total = cond[chunk : chunk + 32, :].astype(jnp.float32)
        weight = in_weight_ref[chunk : chunk + 32, :]
        proj = weight[:, 0:1] * state[0:1, :]
        for latent in range(1, 4):
            proj = proj + weight[:, latent : latent + 1] * state[latent : latent + 1, :]
        raw[slot, chunk : chunk + 32, :] = (proj + total).astype(jnp.bfloat16)


def latent_kernel(
    core,
    plane,
    coef_ref,
    noise_ref,
    noise_edge_ref,
    local_ref,
    state_in_ref,
    in_weight_ref,
    cond_ref,
    cond_edge_ref,
    input_ref,
    state_ref,
):
    me = core()
    at = plane()

    rate, scale_now, scale_next = (coef_ref[0, n] for n in range(3))

    def moved(state, noise):
        return rate * (state - scale_now * noise) + scale_next * noise

    @pl.when(at == 0)
    def _():
        for slot, noise_row, cond in (
            (1 - me, noise_ref.at[0], cond_ref.at[0]),
            (2 - me, noise_ref.at[1], cond_ref.at[1]),
            (2 * me, noise_edge_ref, cond_edge_ref),
        ):
            state = moved(state_in_ref[slot], noise_row[...])
            state_ref[slot] = state
            project(slot, state, cond, in_weight_ref, input_ref)

    @pl.when(at != 0)
    def _():
        state_ref[...] = jnp.zeros_like(state_ref)
        state_ref[1] = moved(state_in_ref[1], local_ref[...])


def edge_kernel(edge_ref, out_ref):
    for chunk in range(0, 320, 64):
        out_ref[chunk : chunk + 64, :] = swish(edge_ref[chunk : chunk + 64, :])


def step_kernel(
    step,
    core,
    plane,
    coef_ref,
    edge_ref,
    rec_ref,
    input_ref,
    state_in_ref,
    in_weight_ref,
    out_weight_ref,
    mine_ref,
    other_ref,
    out_ref,
    state_ref,
    final_ref,
    raw,
    active,
    sums,
):
    me = core()
    at = plane()
    lanes = lax.broadcasted_iota(jnp.int32, (1, 2 * FRAME), 1)
    inside = (lanes % FRAME) < 240

    def activate(slot, rows):
        start = pl.multiple_of(slot * 256, 256)
        tail = pl.multiple_of(768 + slot * 64, 64)
        for chunk in range(0, 320, 64):
            place = start + chunk if chunk < 256 else tail
            active[pl.ds(place, 64), :] = rows(chunk)

    @pl.when(at == 0)
    def _():
        if step == 0:
            extra = edge_ref[320:336, :].astype(jnp.float32)
            halo = (extra[0:4] + extra[4:8]) + extra[8:12]
            halo = jnp.concatenate([halo, jnp.zeros_like(halo)], axis=0)
            for slot, state, cond in (
                (1 - me, state_in_ref[0], rec_ref.at[0]),
                (2 - me, state_in_ref[1], rec_ref.at[1]),
                (2 * me, halo, edge_ref),
            ):
                state_ref[slot] = state
                project(slot, state, cond, in_weight_ref, raw)
        else:
            raw[...] = input_ref[...]
        for slot in range(3):
            activate(slot, lambda chunk, slot=slot: swish(raw[slot, chunk : chunk + 64, :]))

    @pl.when(at != 0)
    def _():
        if step == 0:
            state_ref[...] = jnp.zeros_like(state_ref)
            state_ref[1] = state_in_ref[me]
        raw[1] = rec_ref[me]
        for row in range(2):
            activate(row + 1 - me, lambda chunk, row=row: swish(rec_ref[row, chunk : chunk + 64, :]))
        activate(2 * me, lambda chunk: swish(edge_ref[chunk : chunk + 64, :]))

    for half, weight in enumerate((mine_ref, other_ref)):
        offset = me * 160 if half == 0 else (1 - me) * 160
        sums[...] = jnp.dot(weight[...], active[...], preferred_element_type=jnp.float32)
        for chunk in range(0, 160, 32):
            channels = pl.ds(pl.multiple_of(offset + chunk, 32), 32)
            total = sums[160 + chunk : 160 + chunk + 32, :]
            total = total + pltpu.roll(sums[chunk : chunk + 32, :], 1, axis=1)
            total = total + pltpu.roll(sums[320 + chunk : 320 + chunk + 32, :], 2 * FRAME - 1, axis=1)
            total = total + raw[1, channels, :].astype(jnp.float32)
            out_ref[channels, :] = jnp.where(inside, total, 0.0).astype(jnp.bfloat16)

    if step > 0:
        state_ref[...] = state_in_ref[...]
    final_ref[...] = jnp.zeros_like(final_ref)

    @pl.when(at == 3)
    def _():
        noise = jnp.dot(out_weight_ref[...], out_ref[...], preferred_element_type=jnp.float32)[0:8]
        if step == STEPS - 1:
            rate, scale_now, scale_next = (coef_ref[1, n] for n in range(3))
            noise = rate * (state_in_ref[1] - scale_now * noise) + scale_next * noise
        final_ref[...] = noise


def prepare(feats, latent):
    core = functools.partial(lax.axis_index, "cores")
    return pl.pallas_call(
        functools.partial(prepare_kernel, core),
        out_shape=[
            jax.ShapeDtypeStruct((2, 320, 2 * FRAME), jnp.bfloat16),
            jax.ShapeDtypeStruct((320 + MESSAGE_EXTRA, 2 * FRAME), jnp.bfloat16),
            jax.ShapeDtypeStruct((2, 8, 2 * FRAME), jnp.float32),
        ],
        in_specs=[in_vmem(), pl.BlockSpec(memory_space=pl.ANY)],
        out_specs=[in_vmem()] * 3,
        scratch_shapes=[pltpu.VMEM(latent.shape, latent.dtype), pltpu.SemaphoreType.DMA],
        compiler_params=params(),
        name="prepare",
    )(feats, latent)


def relaid_weight(weight):
    flat = lax.optimization_barrier(weight.astype(jnp.float32)).reshape(-1, LANES)
    return pl.pallas_call(
        weight_kernel,
        out_shape=jax.ShapeDtypeStruct((480, 960), jnp.bfloat16),
        in_specs=[in_vmem()],
        out_specs=in_vmem(),
        scratch_shapes=[pltpu.VMEM((8, 160, LANES), jnp.float32)],
        compiler_params=params(),
        name="relay",
    )(flat)


def hint(micros):
    return pl.CostEstimate(flops=int(micros * 1e9), bytes_accessed=0, transcendentals=0)


def run_latent(coefs, noise, noise_edge, local, state, in_weight, cond, cond_edge):
    core = functools.partial(lax.axis_index, "cores")
    plane = functools.partial(lax.axis_index, "comp")
    return pl.pallas_call(
        functools.partial(latent_kernel, core, plane),
        out_shape=[
            jax.ShapeDtypeStruct((3, 320, 2 * FRAME), jnp.bfloat16),
            jax.ShapeDtypeStruct((3, 8, 2 * FRAME), jnp.float32),
        ],
        in_specs=[pl.BlockSpec(memory_space=pltpu.SMEM)] + [in_vmem()] * 7,
        out_specs=[in_vmem()] * 2,
        compiler_params=params(),
        cost_estimate=hint(3),
        name="latent",
    )(coefs, noise, noise_edge, local, state, in_weight, cond, cond_edge)


def run_edge(edge):
    return pl.pallas_call(
        edge_kernel,
        out_shape=jax.ShapeDtypeStruct((320, 2 * FRAME), jnp.bfloat16),
        in_specs=[in_vmem()],
        out_specs=in_vmem(),
        compiler_params=params(),
        cost_estimate=hint(20),
        name="edge",
    )(edge)


def run_step(step, coefs, rec, edge, inputs, state, in_weight, out_weight, mine, other):
    core = functools.partial(lax.axis_index, "cores")
    plane = functools.partial(lax.axis_index, "comp")
    return pl.pallas_call(
        functools.partial(step_kernel, step, core, plane),
        out_shape=[
            jax.ShapeDtypeStruct((320, 2 * FRAME), jnp.bfloat16),
            jax.ShapeDtypeStruct((3, 8, 2 * FRAME), jnp.float32),
            jax.ShapeDtypeStruct((8, 2 * FRAME), jnp.float32),
        ],
        in_specs=[pl.BlockSpec(memory_space=pltpu.SMEM)] + [in_vmem()] * 8,
        out_specs=[in_vmem()] * 3,
        scratch_shapes=[
            pltpu.VMEM((3, 320, 2 * FRAME), jnp.bfloat16),
            pltpu.VMEM((960, 2 * FRAME), jnp.bfloat16),
            pltpu.VMEM((480, 2 * FRAME), jnp.float32),
        ],
        compiler_params=params(),
        name=f"step{step}",
    )(coefs, edge, rec, inputs, state, in_weight, out_weight, mine, other)


def copy_kernel(in_ref, out_ref):
    out_ref[...] = in_ref[...]


def copied(row):
    return pl.pallas_call(
        copy_kernel,
        out_shape=jax.ShapeDtypeStruct(row.shape, row.dtype),
        in_specs=[in_vmem()],
        out_specs=in_vmem(),
        compiler_params=params(),
        cost_estimate=hint(20),
        name="copy_row",
    )(row)


def links(comps, bands):
    def index(comp, band, core):
        return (comp * bands + band) * 2 + core

    edges, swap = [], []
    onward, diagonals = [], []
    noise_onward, noise_diagonals = [], []
    noise_first, noise_second = [], []
    for comp in range(comps):
        last = comp == comps - 1
        later = 0 if last else comp + 1
        for band in range(bands):
            for core in range(2):
                me = index(comp, band, core)
                (noise_onward if last else onward).append((me, index(later, band, core)))
                if last:
                    noise_first.append((me, index(1, band, core)))
                    noise_second.append((me, index(2, band, core)))
                swap.append((me, index(comp, band, 1 - core)))
                reached = band + 2 * core - 1
                if 0 <= reached < bands:
                    edges.append((me, index(comp, reached, 1 - core)))
                    pair = (me, index(later, reached, 1 - core))
                    (noise_diagonals if last else diagonals).append(pair)
    return edges, swap, onward, diagonals, noise_onward, noise_diagonals, noise_first, noise_second


def body(latent, section_inputs, in_weight, conv_weight, out_weight, timesteps, plan):
    axes = ("comp", "band", "cores")
    edges, swap, onward, diagonals, noise_onward, noise_diagonals, noise_first, noise_second = links(
        lax.axis_size("comp"), lax.axis_size("band")
    )
    plane = lax.axis_index("comp")
    core = lax.axis_index("cores")

    feats = section_inputs[0].reshape(2, 2, 160, 240)
    feats = lax.all_gather(feats, "cores")
    cond, message, state = prepare(feats, latent)
    conv_weight, message = lax.optimization_barrier((conv_weight, message))
    cond_edge = lax.ppermute(message, axes, edges)

    mine = relaid_weight(conv_weight)
    other = lax.ppermute(mine, axes, swap)
    small = jnp.concatenate([in_weight, out_weight.T.astype(jnp.float32)], axis=0)
    small = lax.all_gather(small, "cores")
    in_columns = jnp.concatenate([small[0, 0:4], small[1, 0:4]], axis=1).T
    in_columns = jnp.pad(in_columns, ((0, 0), (0, 4)))
    out_rows = jnp.concatenate([small[0, 4:8], small[1, 4:8]], axis=1)
    out_rows = jnp.pad(out_rows, ((0, 12), (0, 0))).astype(jnp.bfloat16)

    alphas = plan[timesteps]
    rates = jnp.sqrt(alphas[1:] / alphas[:-1])
    scales = jnp.sqrt(1.0 - alphas)
    coefs = jnp.stack([rates, scales[:-1], scales[1:]], axis=1)

    rec, edge = cond, cond_edge
    inputs = jnp.zeros((3, 16, LANES), jnp.bfloat16)
    for step in range(STEPS):
        pair = coefs[max(step - 1, 0) : max(step - 1, 0) + 2]
        out, state, final = run_step(step, pair, rec, edge, inputs, state, in_columns, out_rows, mine, other)
        if step + 1 < STEPS:
            edge = lax.ppermute(out, axes, diagonals)
            rec = lax.ppermute(out, axes, onward)
            rec = lax.all_gather(rec, "cores")
            noise = lax.all_gather(lax.ppermute(final, axes, noise_onward), "cores")
            noise_edge = lax.ppermute(final, axes, noise_diagonals)
            state = copied(state)
            inputs, state = run_latent(
                coefs[step : step + 2],
                noise,
                noise_edge,
                final,
                state,
                in_columns,
                cond,
                cond_edge,
            )

    whole = lax.all_gather(out, "cores")
    share = lax.dynamic_slice_in_dim(whole, core * 160, 160, axis=1)
    share = share.reshape(2, 160, 2, FRAME)[..., :240].transpose(2, 0, 1, 3)
    handoff = share.reshape(1, 2, 2, 160 * 240)

    total = final
    for pairs in (noise_onward, noise_first, noise_second):
        total = total + lax.ppermute(final, axes, pairs)
    total = lax.all_gather(lax.dynamic_slice_in_dim(total, plane, 1, axis=0)[0], "cores")
    denoised = total.reshape(2, 2, FRAME)[..., :240].transpose(1, 0, 2)[:, None]
    return denoised, handoff


def solution(mesh):
    in_specs = (
        P(None, None, "band", None),
        P("comp", None, "band", "cores"),
        P(None, "cores"),
        P("comp", "cores"),
        P("cores", None),
        P(),
        P(),
    )
    out_specs = (P(None, "comp", "band", None), P("comp", None, "band", "cores"))
    return jax.shard_map(body, mesh=mesh, in_specs=in_specs, out_specs=out_specs, check_vma=False)
```

```python
import functools

import jax
import jax.numpy as jnp
from jax import lax
from jax.experimental import pallas as pl
from jax.experimental.pallas import tpu as pltpu
from jax.sharding import PartitionSpec as P

STEPS = 3
TAPS = 3
LANES = 128
FRAME = 256
MESSAGE_EXTRA = 16
VMEM_BYTES = 14 * 1024 * 1024


def params():
    return pltpu.CompilerParams(vmem_limit_bytes=VMEM_BYTES)


def in_vmem():
    return pl.BlockSpec(memory_space=pltpu.VMEM)


def weight_kernel(flat_ref, out_ref, held):
    lane = lax.broadcasted_iota(jnp.int32, (80, LANES), 1)
    low = lane < 64

    def rows(start):
        return flat_ref[pl.ds(start, 80, stride=45), :]

    def swapped(value):
        return pltpu.roll(value, 64, axis=1)

    for dq in range(TAPS):
        for parity in range(2):
            tails = []
            for dr in range(TAPS):
                start = 45 * parity + 5 * (3 * dr + dq)
                place, half = start // 2, start % 2
                first, second, third = (rows(place + n) for n in range(3))
                if half:
                    one = swapped(jnp.where(low, second, first))
                    two = swapped(jnp.where(low, third, second))
                    tail_low = False
                else:
                    one, two = first, second
                    tail_low = True
                held[2 * dr, pl.ds(parity, 80, stride=2), :] = one
                held[2 * dr + 1, pl.ds(parity, 80, stride=2), :] = two
                wants_low = dr != 1
                tails.append(third if tail_low == wants_low else swapped(third))
            held[6, pl.ds(parity, 80, stride=2), :] = jnp.where(low, tails[0], tails[1])
            held[7, pl.ds(parity, 80, stride=2), :] = tails[2]
        at = dq * 160
        for tile in range(7):
            out_ref[at : at + 160, tile * LANES : (tile + 1) * LANES] = held[tile].astype(jnp.bfloat16)
        out_ref[at : at + 160, 896:960] = held[7, :, :64].astype(jnp.bfloat16)


def prepare_kernel(core, feat_ref, latent_ref, own_ref, message_ref, state_ref, latent, sem):
    copy = pltpu.make_async_copy(latent_ref, latent, sem)
    copy.start()
    own_ref[...] = jnp.zeros_like(own_ref)
    state_ref[...] = jnp.zeros_like(state_ref)
    for half in range(2):
        for frame in range(2):
            for row in range(2):
                own_ref[row, half * 160 : half * 160 + 160, frame * FRAME : frame * FRAME + 240] = feat_ref[
                    half, frame, row
                ]
    me = core()
    message_ref[0:320, :] = own_ref[me]
    copy.wait()
    for frame in range(2):
        for row in range(2):
            state_ref[row, 0:4, frame * FRAME : frame * FRAME + 240] = latent[frame, :, row, :]
    state = state_ref[me, 0:4, :]
    high = state.astype(jnp.bfloat16).astype(jnp.float32)
    left = state - high
    middle = left.astype(jnp.bfloat16).astype(jnp.float32)
    low = left - middle
    parts = jnp.concatenate([high, middle, low, jnp.zeros_like(low)], axis=0)
    message_ref[320:336, :] = parts.astype(jnp.bfloat16)


def swish(value):
    value = value.astype(jnp.float32)
    return (0.5 * value * (1.0 + jnp.tanh(0.5 * value))).astype(jnp.bfloat16)


def project(slot, state, cond, in_weight_ref, raw):
    for chunk in range(0, 320, 32):
        total = cond[chunk : chunk + 32, :].astype(jnp.float32)
        weight = in_weight_ref[chunk : chunk + 32, :]
        proj = weight[:, 0:1] * state[0:1, :]
        for latent in range(1, 4):
            proj = proj + weight[:, latent : latent + 1] * state[latent : latent + 1, :]
        raw[slot, chunk : chunk + 32, :] = (proj + total).astype(jnp.bfloat16)


def latent_kernel(
    core,
    plane,
    coef_ref,
    noise_ref,
    noise_edge_ref,
    local_ref,
    state_in_ref,
    in_weight_ref,
    cond_ref,
    cond_edge_ref,
    input_ref,
    state_ref,
):
    me = core()
    at = plane()

    rate, scale_now, scale_next = (coef_ref[0, n] for n in range(3))

    def moved(state, noise):
        return rate * (state - scale_now * noise) + scale_next * noise

    @pl.when(at == 0)
    def _():
        for slot, noise_row, cond in (
            (1 - me, noise_ref.at[0], cond_ref.at[0]),
            (2 - me, noise_ref.at[1], cond_ref.at[1]),
            (2 * me, noise_edge_ref, cond_edge_ref),
        ):
            state = moved(state_in_ref[slot], noise_row[...])
            state_ref[slot] = state
            project(slot, state, cond, in_weight_ref, input_ref)

    @pl.when(at != 0)
    def _():
        state_ref[...] = jnp.zeros_like(state_ref)
        state_ref[1] = moved(state_in_ref[1], local_ref[...])


def edge_kernel(edge_ref, out_ref):
    for chunk in range(0, 320, 64):
        out_ref[chunk : chunk + 64, :] = swish(edge_ref[chunk : chunk + 64, :])


def step_kernel(
    step,
    core,
    plane,
    coef_ref,
    input_ref,
    state_in_ref,
    edge_ref,
    rec_ref,
    in_weight_ref,
    out_weight_ref,
    mine_ref,
    other_ref,
    out_ref,
    state_ref,
    final_ref,
    raw,
    active,
    sums,
):
    me = core()
    at = plane()
    lanes = lax.broadcasted_iota(jnp.int32, (1, 2 * FRAME), 1)
    inside = (lanes % FRAME) < 240

    def activate(slot, rows):
        start = pl.multiple_of(slot * 256, 256)
        tail = pl.multiple_of(768 + slot * 64, 64)
        for chunk in range(0, 320, 64):
            place = start + chunk if chunk < 256 else tail
            active[pl.ds(place, 64), :] = rows(chunk)

    @pl.when(at == 0)
    def _():
        if step == 0:
            extra = edge_ref[320:336, :].astype(jnp.float32)
            halo = (extra[0:4] + extra[4:8]) + extra[8:12]
            halo = jnp.concatenate([halo, jnp.zeros_like(halo)], axis=0)
            for slot, state, cond in (
                (1 - me, state_in_ref[0], rec_ref.at[0]),
                (2 - me, state_in_ref[1], rec_ref.at[1]),
                (2 * me, halo, edge_ref),
            ):
                state_ref[slot] = state
                project(slot, state, cond, in_weight_ref, raw)
        else:
            raw[...] = input_ref[...]
        for slot in range(3):
            activate(slot, lambda chunk, slot=slot: swish(raw[slot, chunk : chunk + 64, :]))

    @pl.when(at != 0)
    def _():
        if step == 0:
            state_ref[...] = jnp.zeros_like(state_ref)
            state_ref[1] = state_in_ref[me]
        raw[1] = rec_ref[me]
        for row in range(2):
            activate(row + 1 - me, lambda chunk, row=row: swish(rec_ref[row, chunk : chunk + 64, :]))
        activate(2 * me, lambda chunk: swish(edge_ref[chunk : chunk + 64, :]))

    for half, weight in enumerate((mine_ref, other_ref)):
        offset = me * 160 if half == 0 else (1 - me) * 160
        sums[...] = jnp.dot(weight[...], active[...], preferred_element_type=jnp.float32)
        for chunk in range(0, 160, 32):
            channels = pl.ds(pl.multiple_of(offset + chunk, 32), 32)
            total = sums[160 + chunk : 160 + chunk + 32, :]
            total = total + pltpu.roll(sums[chunk : chunk + 32, :], 1, axis=1)
            total = total + pltpu.roll(sums[320 + chunk : 320 + chunk + 32, :], 2 * FRAME - 1, axis=1)
            total = total + raw[1, channels, :].astype(jnp.float32)
            out_ref[channels, :] = jnp.where(inside, total, 0.0).astype(jnp.bfloat16)

    if 0 < step < STEPS - 1:
        state_ref[...] = state_in_ref[...]
    final_ref[...] = jnp.zeros_like(final_ref)

    @pl.when(at == 3)
    def _():
        noise = jnp.dot(out_weight_ref[...], out_ref[...], preferred_element_type=jnp.float32)[0:8]
        if step == STEPS - 1:
            rate, scale_now, scale_next = (coef_ref[1, n] for n in range(3))
            noise = rate * (state_in_ref[1] - scale_now * noise) + scale_next * noise
        final_ref[...] = noise


def prepare(feats, latent):
    core = functools.partial(lax.axis_index, "cores")
    return pl.pallas_call(
        functools.partial(prepare_kernel, core),
        out_shape=[
            jax.ShapeDtypeStruct((2, 320, 2 * FRAME), jnp.bfloat16),
            jax.ShapeDtypeStruct((320 + MESSAGE_EXTRA, 2 * FRAME), jnp.bfloat16),
            jax.ShapeDtypeStruct((2, 8, 2 * FRAME), jnp.float32),
        ],
        in_specs=[in_vmem(), pl.BlockSpec(memory_space=pl.ANY)],
        out_specs=[in_vmem()] * 3,
        scratch_shapes=[pltpu.VMEM(latent.shape, latent.dtype), pltpu.SemaphoreType.DMA],
        compiler_params=params(),
        name="prepare",
    )(feats, latent)


def relaid_weight(weight):
    flat = lax.optimization_barrier(weight.astype(jnp.float32)).reshape(-1, LANES)
    return pl.pallas_call(
        weight_kernel,
        out_shape=jax.ShapeDtypeStruct((480, 960), jnp.bfloat16),
        in_specs=[in_vmem()],
        out_specs=in_vmem(),
        scratch_shapes=[pltpu.VMEM((8, 160, LANES), jnp.float32)],
        compiler_params=params(),
        name="relay",
    )(flat)


def hint(micros):
    return pl.CostEstimate(flops=int(micros * 1e9), bytes_accessed=0, transcendentals=0)


def run_latent(coefs, noise, noise_edge, local, state, in_weight, cond, cond_edge):
    core = functools.partial(lax.axis_index, "cores")
    plane = functools.partial(lax.axis_index, "comp")
    return pl.pallas_call(
        functools.partial(latent_kernel, core, plane),
        out_shape=[
            jax.ShapeDtypeStruct((3, 320, 2 * FRAME), jnp.bfloat16),
            jax.ShapeDtypeStruct((3, 8, 2 * FRAME), jnp.float32),
        ],
        in_specs=[pl.BlockSpec(memory_space=pltpu.SMEM)] + [in_vmem()] * 7,
        out_specs=[in_vmem()] * 2,
        compiler_params=params(),
        cost_estimate=hint(3),
        name="latent",
    )(coefs, noise, noise_edge, local, state, in_weight, cond, cond_edge)


def run_edge(edge):
    return pl.pallas_call(
        edge_kernel,
        out_shape=jax.ShapeDtypeStruct((320, 2 * FRAME), jnp.bfloat16),
        in_specs=[in_vmem()],
        out_specs=in_vmem(),
        compiler_params=params(),
        cost_estimate=hint(20),
        name="edge",
    )(edge)


def run_step(step, coefs, rec, edge, inputs, state, in_weight, out_weight, mine, other):
    core = functools.partial(lax.axis_index, "cores")
    plane = functools.partial(lax.axis_index, "comp")
    return pl.pallas_call(
        functools.partial(step_kernel, step, core, plane),
        out_shape=[
            jax.ShapeDtypeStruct((320, 2 * FRAME), jnp.bfloat16),
            jax.ShapeDtypeStruct((3 if step < STEPS - 1 else 1, 8, 2 * FRAME), jnp.float32),
            jax.ShapeDtypeStruct((8, 2 * FRAME), jnp.float32),
        ],
        in_specs=[pl.BlockSpec(memory_space=pltpu.SMEM)] + [in_vmem()] * 8,
        out_specs=[in_vmem()] * 3,
        scratch_shapes=[
            pltpu.VMEM((3, 320, 2 * FRAME), jnp.bfloat16),
            pltpu.VMEM((960, 2 * FRAME), jnp.bfloat16),
            pltpu.VMEM((480, 2 * FRAME), jnp.float32),
        ],
        compiler_params=params(),
        name=f"step{step}",
    )(coefs, inputs, state, edge, rec, in_weight, out_weight, mine, other)


def copy_kernel(in_ref, out_ref):
    out_ref[...] = in_ref[...]


def copied(row):
    return pl.pallas_call(
        copy_kernel,
        out_shape=jax.ShapeDtypeStruct(row.shape, row.dtype),
        in_specs=[in_vmem()],
        out_specs=in_vmem(),
        compiler_params=params(),
        cost_estimate=hint(20),
        name="copy_row",
    )(row)


def arrange_kernel(small_ref, columns_ref, rows_ref):
    rows_ref[...] = jnp.zeros_like(rows_ref)
    for half in range(2):
        value = small_ref[half]
        filled = jnp.concatenate([value, jnp.zeros((8, 96), jnp.float32)], axis=1)
        columns_ref[half * 160 : half * 160 + 160, :] = filled.T[0:160]
    whole = jnp.concatenate([small_ref[0], small_ref[1]], axis=1)
    rows_ref[0:4, :] = whole[4:8].astype(jnp.bfloat16)


def arranged(small):
    return pl.pallas_call(
        arrange_kernel,
        out_shape=[jax.ShapeDtypeStruct((320, 8), jnp.float32), jax.ShapeDtypeStruct((16, 320), jnp.bfloat16)],
        in_specs=[in_vmem()],
        out_specs=[in_vmem()] * 2,
        compiler_params=params(),
        name="arrange",
    )(small)


def links(comps, bands):
    def index(comp, band, core):
        return (comp * bands + band) * 2 + core

    edges, swap = [], []
    onward, diagonals = [], []
    noise_onward, noise_diagonals = [], []
    noise_first, noise_second = [], []
    for comp in range(comps):
        last = comp == comps - 1
        later = 0 if last else comp + 1
        for band in range(bands):
            for core in range(2):
                me = index(comp, band, core)
                (noise_onward if last else onward).append((me, index(later, band, core)))
                if last:
                    noise_first.append((me, index(1, band, core)))
                    noise_second.append((me, index(2, band, core)))
                swap.append((me, index(comp, band, 1 - core)))
                reached = band + 2 * core - 1
                if 0 <= reached < bands:
                    edges.append((me, index(comp, reached, 1 - core)))
                    pair = (me, index(later, reached, 1 - core))
                    (noise_diagonals if last else diagonals).append(pair)
    return edges, swap, onward, diagonals, noise_onward, noise_diagonals, noise_first, noise_second


def body(latent, section_inputs, in_weight, conv_weight, out_weight, timesteps, plan):
    axes = ("comp", "band", "cores")
    edges, swap, onward, diagonals, noise_onward, noise_diagonals, noise_first, noise_second = links(
        lax.axis_size("comp"), lax.axis_size("band")
    )
    plane = lax.axis_index("comp")
    core = lax.axis_index("cores")

    feats = section_inputs[0].reshape(2, 2, 160, 240)
    feats = lax.all_gather(feats, "cores")
    cond, message, state = prepare(feats, latent)
    conv_weight, message = lax.optimization_barrier((conv_weight, message))
    cond_edge = lax.ppermute(message, axes, edges)

    mine = relaid_weight(conv_weight)
    other = lax.ppermute(mine, axes, swap)
    small = jnp.concatenate([in_weight, out_weight.T.astype(jnp.float32)], axis=0)
    small = lax.all_gather(small, "cores")
    in_columns, out_rows = arranged(small)

    alphas = plan[timesteps]
    rates = jnp.sqrt(alphas[1:] / alphas[:-1])
    scales = jnp.sqrt(1.0 - alphas)
    coefs = jnp.stack([rates, scales[:-1], scales[1:]], axis=1)

    rec, edge = cond, cond_edge
    inputs = jnp.zeros((3, 16, LANES), jnp.bfloat16)
    for step in range(STEPS):
        pair = coefs[max(step - 1, 0) : max(step - 1, 0) + 2]
        out, state, final = run_step(step, pair, rec, edge, inputs, state, in_columns, out_rows, mine, other)
        if step + 1 < STEPS:
            edge = lax.ppermute(out, axes, diagonals)
            rec = lax.ppermute(out, axes, onward)
            rec = lax.all_gather(rec, "cores")
            noise = lax.all_gather(lax.ppermute(final, axes, noise_onward), "cores")
            noise_edge = lax.ppermute(final, axes, noise_diagonals)
            state = copied(state)
            inputs, state = run_latent(
                coefs[step : step + 2],
                noise,
                noise_edge,
                final,
                state,
                in_columns,
                cond,
                cond_edge,
            )

    whole = lax.all_gather(out, "cores")
    share = lax.dynamic_slice_in_dim(whole, core * 160, 160, axis=1)
    share = share.reshape(2, 160, 2, FRAME)[..., :240].transpose(2, 0, 1, 3)
    handoff = share.reshape(1, 2, 2, 160 * 240)

    total = final
    for pairs in (noise_second, noise_first, noise_onward):
        total = total + lax.ppermute(final, axes, pairs)
    total = lax.all_gather(lax.dynamic_slice_in_dim(total, plane, 1, axis=0)[0], "cores")
    denoised = total.reshape(2, 2, FRAME)[..., :240].transpose(1, 0, 2)[:, None]
    return denoised, handoff


def solution(mesh):
    in_specs = (
        P(None, None, "band", None),
        P("comp", None, "band", "cores"),
        P(None, "cores"),
        P("comp", "cores"),
        P("cores", None),
        P(),
        P(),
    )
    out_specs = (P(None, "comp", "band", None), P("comp", None, "band", "cores"))
    return jax.shard_map(body, mesh=mesh, in_specs=in_specs, out_specs=out_specs, check_vma=False)
```

```python
import functools

import jax
import jax.numpy as jnp
from jax import lax
from jax.experimental import pallas as pl
from jax.experimental.pallas import tpu as pltpu
from jax.sharding import PartitionSpec as P

STEPS = 3
TAPS = 3
LANES = 128
FRAME = 256
MESSAGE_EXTRA = 16
VMEM_BYTES = 14 * 1024 * 1024


def params():
    return pltpu.CompilerParams(vmem_limit_bytes=VMEM_BYTES)


def in_vmem():
    return pl.BlockSpec(memory_space=pltpu.VMEM)


def weight_kernel(flat_ref, out_ref, held):
    lane = lax.broadcasted_iota(jnp.int32, (80, LANES), 1)
    low = lane < 64

    def rows(start):
        return flat_ref[pl.ds(start, 80, stride=45), :]

    def swapped(value):
        return pltpu.roll(value, 64, axis=1)

    for dq in range(TAPS):
        for parity in range(2):
            tails = []
            for dr in range(TAPS):
                start = 45 * parity + 5 * (3 * dr + dq)
                place, half = start // 2, start % 2
                first, second, third = (rows(place + n) for n in range(3))
                if half:
                    one = swapped(jnp.where(low, second, first))
                    two = swapped(jnp.where(low, third, second))
                    tail_low = False
                else:
                    one, two = first, second
                    tail_low = True
                held[2 * dr, pl.ds(parity, 80, stride=2), :] = one
                held[2 * dr + 1, pl.ds(parity, 80, stride=2), :] = two
                wants_low = dr != 1
                tails.append(third if tail_low == wants_low else swapped(third))
            held[6, pl.ds(parity, 80, stride=2), :] = jnp.where(low, tails[0], tails[1])
            held[7, pl.ds(parity, 80, stride=2), :] = tails[2]
        at = dq * 160
        for tile in range(7):
            out_ref[at : at + 160, tile * LANES : (tile + 1) * LANES] = held[tile].astype(jnp.bfloat16)
        out_ref[at : at + 160, 896:960] = held[7, :, :64].astype(jnp.bfloat16)


def prepare_kernel(core, feat_ref, latent_ref, own_ref, message_ref, state_ref, latent, sem):
    copy = pltpu.make_async_copy(latent_ref, latent, sem)
    copy.start()
    own_ref[...] = jnp.zeros_like(own_ref)
    state_ref[...] = jnp.zeros_like(state_ref)
    for half in range(2):
        for frame in range(2):
            for row in range(2):
                own_ref[row, half * 160 : half * 160 + 160, frame * FRAME : frame * FRAME + 240] = feat_ref[
                    half, frame, row
                ]
    me = core()
    message_ref[0:320, :] = own_ref[me]
    copy.wait()
    for frame in range(2):
        for row in range(2):
            state_ref[row, 0:4, frame * FRAME : frame * FRAME + 240] = latent[frame, :, row, :]
    state = state_ref[me, 0:4, :]
    high = state.astype(jnp.bfloat16).astype(jnp.float32)
    left = state - high
    middle = left.astype(jnp.bfloat16).astype(jnp.float32)
    low = left - middle
    parts = jnp.concatenate([high, middle, low, jnp.zeros_like(low)], axis=0)
    message_ref[320:336, :] = parts.astype(jnp.bfloat16)


def swish(value):
    value = value.astype(jnp.float32)
    return (0.5 * value * (1.0 + jnp.tanh(0.5 * value))).astype(jnp.bfloat16)


def project(slot, state, cond, in_weight_ref, raw):
    for chunk in range(0, 320, 32):
        total = cond[chunk : chunk + 32, :].astype(jnp.float32)
        weight = in_weight_ref[chunk : chunk + 32, :]
        proj = weight[:, 0:1] * state[0:1, :]
        for latent in range(1, 4):
            proj = proj + weight[:, latent : latent + 1] * state[latent : latent + 1, :]
        raw[slot, chunk : chunk + 32, :] = (proj + total).astype(jnp.bfloat16)


def latent_kernel(
    core,
    plane,
    coef_ref,
    noise_ref,
    noise_edge_ref,
    local_ref,
    state_in_ref,
    in_weight_ref,
    cond_ref,
    cond_edge_ref,
    input_ref,
    state_ref,
):
    me = core()
    at = plane()

    rate, scale_now, scale_next = (coef_ref[0, n] for n in range(3))

    def moved(state, noise):
        return rate * (state - scale_now * noise) + scale_next * noise

    @pl.when(at == 0)
    def _():
        for slot, noise_row, cond in (
            (1 - me, noise_ref.at[0], cond_ref.at[0]),
            (2 - me, noise_ref.at[1], cond_ref.at[1]),
            (2 * me, noise_edge_ref, cond_edge_ref),
        ):
            state = moved(state_in_ref[slot], noise_row[...])
            state_ref[slot] = state
            project(slot, state, cond, in_weight_ref, input_ref)

    @pl.when(at != 0)
    def _():
        state_ref[...] = jnp.zeros_like(state_ref)
        state_ref[1] = moved(state_in_ref[1], local_ref[...])


def edge_kernel(edge_ref, out_ref):
    for chunk in range(0, 320, 64):
        out_ref[chunk : chunk + 64, :] = swish(edge_ref[chunk : chunk + 64, :])


def step_kernel(
    step,
    core,
    plane,
    coef_ref,
    input_ref,
    state_in_ref,
    edge_ref,
    rec_ref,
    in_weight_ref,
    out_weight_ref,
    mine_ref,
    other_ref,
    out_ref,
    *rest,
):
    *kept, final_ref, raw, active, sums = rest
    state_ref = kept[0] if kept else None
    me = core()
    at = plane()
    lanes = lax.broadcasted_iota(jnp.int32, (1, 2 * FRAME), 1)
    inside = (lanes % FRAME) < 240

    def activate(slot, rows):
        start = pl.multiple_of(slot * 256, 256)
        tail = pl.multiple_of(768 + slot * 64, 64)
        for chunk in range(0, 320, 64):
            place = start + chunk if chunk < 256 else tail
            active[pl.ds(place, 64), :] = rows(chunk)

    @pl.when(at == 0)
    def _():
        if step == 0:
            extra = edge_ref[320:336, :].astype(jnp.float32)
            halo = (extra[0:4] + extra[4:8]) + extra[8:12]
            halo = jnp.concatenate([halo, jnp.zeros_like(halo)], axis=0)
            for slot, state, cond in (
                (1 - me, state_in_ref[0], rec_ref.at[0]),
                (2 - me, state_in_ref[1], rec_ref.at[1]),
                (2 * me, halo, edge_ref),
            ):
                state_ref[slot] = state
                project(slot, state, cond, in_weight_ref, raw)
        else:
            raw[...] = input_ref[...]
        for slot in range(3):
            activate(slot, lambda chunk, slot=slot: swish(raw[slot, chunk : chunk + 64, :]))

    @pl.when(at != 0)
    def _():
        if step == 0:
            state_ref[...] = jnp.zeros_like(state_ref)
            state_ref[1] = state_in_ref[me]
        raw[1] = rec_ref[me]
        for row in range(2):
            activate(row + 1 - me, lambda chunk, row=row: swish(rec_ref[row, chunk : chunk + 64, :]))
        activate(2 * me, lambda chunk: swish(edge_ref[chunk : chunk + 64, :]))

    for half, weight in enumerate((mine_ref, other_ref)):
        offset = me * 160 if half == 0 else (1 - me) * 160
        sums[...] = jnp.dot(weight[...], active[...], preferred_element_type=jnp.float32)
        for chunk in range(0, 160, 32):
            channels = pl.ds(pl.multiple_of(offset + chunk, 32), 32)
            total = sums[160 + chunk : 160 + chunk + 32, :]
            total = total + pltpu.roll(sums[chunk : chunk + 32, :], 1, axis=1)
            total = total + pltpu.roll(sums[320 + chunk : 320 + chunk + 32, :], 2 * FRAME - 1, axis=1)
            total = total + raw[1, channels, :].astype(jnp.float32)
            out_ref[channels, :] = jnp.where(inside, total, 0.0).astype(jnp.bfloat16)

    if 0 < step < STEPS - 1:
        state_ref[...] = state_in_ref[...]
    final_ref[...] = jnp.zeros_like(final_ref)

    @pl.when(at == 3)
    def _():
        noise = jnp.dot(out_weight_ref[...], out_ref[...], preferred_element_type=jnp.float32)[0:8]
        if step == STEPS - 1:
            rate, scale_now, scale_next = (coef_ref[1, n] for n in range(3))
            noise = rate * (state_in_ref[1] - scale_now * noise) + scale_next * noise
        final_ref[...] = noise


def prepare(feats, latent):
    core = functools.partial(lax.axis_index, "cores")
    return pl.pallas_call(
        functools.partial(prepare_kernel, core),
        out_shape=[
            jax.ShapeDtypeStruct((2, 320, 2 * FRAME), jnp.bfloat16),
            jax.ShapeDtypeStruct((320 + MESSAGE_EXTRA, 2 * FRAME), jnp.bfloat16),
            jax.ShapeDtypeStruct((2, 8, 2 * FRAME), jnp.float32),
        ],
        in_specs=[in_vmem(), pl.BlockSpec(memory_space=pltpu.HBM)],
        out_specs=[in_vmem()] * 3,
        scratch_shapes=[pltpu.VMEM(latent.shape, latent.dtype), pltpu.SemaphoreType.DMA],
        compiler_params=params(),
        name="prepare",
    )(feats, latent)


def relaid_weight(weight):
    flat = lax.optimization_barrier(weight.astype(jnp.float32)).reshape(-1, LANES)
    return pl.pallas_call(
        weight_kernel,
        out_shape=jax.ShapeDtypeStruct((480, 960), jnp.bfloat16),
        in_specs=[in_vmem()],
        out_specs=in_vmem(),
        scratch_shapes=[pltpu.VMEM((8, 160, LANES), jnp.float32)],
        compiler_params=params(),
        name="relay",
    )(flat)


def hint(micros):
    return pl.CostEstimate(flops=int(micros * 1e9), bytes_accessed=0, transcendentals=0)


def run_latent(coefs, noise, noise_edge, local, state, in_weight, cond, cond_edge):
    core = functools.partial(lax.axis_index, "cores")
    plane = functools.partial(lax.axis_index, "comp")
    return pl.pallas_call(
        functools.partial(latent_kernel, core, plane),
        out_shape=[
            jax.ShapeDtypeStruct((3, 320, 2 * FRAME), jnp.bfloat16),
            jax.ShapeDtypeStruct((3, 8, 2 * FRAME), jnp.float32),
        ],
        in_specs=[pl.BlockSpec(memory_space=pltpu.SMEM)] + [in_vmem()] * 7,
        out_specs=[in_vmem()] * 2,
        compiler_params=params(),
        cost_estimate=hint(3),
        name="latent",
    )(coefs, noise, noise_edge, local, state, in_weight, cond, cond_edge)


def run_edge(edge):
    return pl.pallas_call(
        edge_kernel,
        out_shape=jax.ShapeDtypeStruct((320, 2 * FRAME), jnp.bfloat16),
        in_specs=[in_vmem()],
        out_specs=in_vmem(),
        compiler_params=params(),
        cost_estimate=hint(20),
        name="edge",
    )(edge)


def run_step(step, coefs, rec, edge, inputs, state, in_weight, out_weight, mine, other):
    core = functools.partial(lax.axis_index, "cores")
    plane = functools.partial(lax.axis_index, "comp")
    return pl.pallas_call(
        functools.partial(step_kernel, step, core, plane),
        out_shape=[
            jax.ShapeDtypeStruct((320, 2 * FRAME), jnp.bfloat16),
        ]
        + [jax.ShapeDtypeStruct((3, 8, 2 * FRAME), jnp.float32)] * (step < STEPS - 1)
        + [jax.ShapeDtypeStruct((8, 2 * FRAME), jnp.float32)],
        in_specs=[pl.BlockSpec(memory_space=pltpu.SMEM)] + [in_vmem()] * 8,
        out_specs=[in_vmem()] * (3 if step < STEPS - 1 else 2),
        scratch_shapes=[
            pltpu.VMEM((3, 320, 2 * FRAME), jnp.bfloat16),
            pltpu.VMEM((960, 2 * FRAME), jnp.bfloat16),
            pltpu.VMEM((480, 2 * FRAME), jnp.float32),
        ],
        compiler_params=params(),
        name=f"step{step}",
    )(coefs, inputs, state, edge, rec, in_weight, out_weight, mine, other)


def copy_kernel(in_ref, out_ref):
    out_ref[...] = in_ref[...]


def copied(row):
    return pl.pallas_call(
        copy_kernel,
        out_shape=jax.ShapeDtypeStruct(row.shape, row.dtype),
        in_specs=[in_vmem()],
        out_specs=in_vmem(),
        compiler_params=params(),
        cost_estimate=hint(20),
        name="copy_row",
    )(row)


def finish_kernel(rows_ref, out_ref):
    for row in range(2):
        for frame in range(2):
            out_ref[frame, 0, row : row + 1, :] = rows_ref[row : row + 1, frame * FRAME : frame * FRAME + 240]


def finished(rows):
    return pl.pallas_call(
        finish_kernel,
        out_shape=jax.ShapeDtypeStruct((2, 1, 2, 240), jnp.float32),
        in_specs=[in_vmem()],
        out_specs=in_vmem(),
        compiler_params=params(),
        name="finish",
    )(rows)


def arrange_kernel(small_ref, columns_ref, rows_ref):
    rows_ref[...] = jnp.zeros_like(rows_ref)
    for half in range(2):
        value = small_ref[half]
        filled = jnp.concatenate([value, jnp.zeros((8, 96), jnp.float32)], axis=1)
        columns_ref[half * 160 : half * 160 + 160, :] = filled.T[0:160]
    whole = jnp.concatenate([small_ref[0], small_ref[1]], axis=1)
    rows_ref[0:4, :] = whole[4:8].astype(jnp.bfloat16)


def arranged(small):
    return pl.pallas_call(
        arrange_kernel,
        out_shape=[jax.ShapeDtypeStruct((320, 8), jnp.float32), jax.ShapeDtypeStruct((16, 320), jnp.bfloat16)],
        in_specs=[in_vmem()],
        out_specs=[in_vmem()] * 2,
        compiler_params=params(),
        name="arrange",
    )(small)


def links(comps, bands):
    def index(comp, band, core):
        return (comp * bands + band) * 2 + core

    edges, swap = [], []
    onward, diagonals = [], []
    noise_onward, noise_diagonals = [], []
    noise_first, noise_second = [], []
    for comp in range(comps):
        last = comp == comps - 1
        later = 0 if last else comp + 1
        for band in range(bands):
            for core in range(2):
                me = index(comp, band, core)
                (noise_onward if last else onward).append((me, index(later, band, core)))
                if last:
                    noise_first.append((me, index(1, band, core)))
                    noise_second.append((me, index(2, band, core)))
                swap.append((me, index(comp, band, 1 - core)))
                reached = band + 2 * core - 1
                if 0 <= reached < bands:
                    edges.append((me, index(comp, reached, 1 - core)))
                    pair = (me, index(later, reached, 1 - core))
                    (noise_diagonals if last else diagonals).append(pair)
    return edges, swap, onward, diagonals, noise_onward, noise_diagonals, noise_first, noise_second


def body(latent, section_inputs, in_weight, conv_weight, out_weight, timesteps, plan):
    axes = ("comp", "band", "cores")
    edges, swap, onward, diagonals, noise_onward, noise_diagonals, noise_first, noise_second = links(
        lax.axis_size("comp"), lax.axis_size("band")
    )
    plane = lax.axis_index("comp")
    core = lax.axis_index("cores")

    feats = section_inputs[0].reshape(2, 2, 160, 240)
    feats = lax.all_gather(feats, "cores")
    cond, message, state = prepare(feats, latent)
    conv_weight, message = lax.optimization_barrier((conv_weight, message))
    cond_edge = lax.ppermute(message, axes, edges)

    mine = relaid_weight(conv_weight)
    other = lax.ppermute(mine, axes, swap)
    small = jnp.concatenate([in_weight, out_weight.T.astype(jnp.float32)], axis=0)
    small = lax.all_gather(small, "cores")
    in_columns, out_rows = arranged(small)

    alphas = plan[timesteps]
    rates = jnp.sqrt(alphas[1:] / alphas[:-1])
    scales = jnp.sqrt(1.0 - alphas)
    coefs = jnp.stack([rates, scales[:-1], scales[1:]], axis=1)

    rec, edge = cond, cond_edge
    inputs = jnp.zeros((3, 16, LANES), jnp.bfloat16)
    for step in range(STEPS):
        pair = coefs[max(step - 1, 0) : max(step - 1, 0) + 2]
        out, *kept, final = run_step(step, pair, rec, edge, inputs, state, in_columns, out_rows, mine, other)
        if step + 1 < STEPS:
            state = kept[0]
            edge = lax.ppermute(out, axes, diagonals)
            rec = lax.ppermute(out, axes, onward)
            rec = lax.all_gather(rec, "cores")
            noise = lax.all_gather(lax.ppermute(final, axes, noise_onward), "cores")
            noise_edge = lax.ppermute(final, axes, noise_diagonals)
            state = copied(state)
            inputs, state = run_latent(
                coefs[step : step + 2],
                noise,
                noise_edge,
                final,
                state,
                in_columns,
                cond,
                cond_edge,
            )

    whole = lax.all_gather(out, "cores")
    share = lax.dynamic_slice_in_dim(whole, core * 160, 160, axis=1)
    share = share.reshape(2, 160, 2, FRAME)[..., :240].transpose(2, 0, 1, 3)
    handoff = share.reshape(1, 2, 2, 160 * 240)

    total = final
    for pairs in (noise_second, noise_first, noise_onward):
        total = total + lax.ppermute(final, axes, pairs)
    total = lax.all_gather(lax.dynamic_slice_in_dim(total, plane, 1, axis=0)[0], "cores")
    denoised = finished(total)
    return denoised, handoff


def solution(mesh):
    in_specs = (
        P(None, None, "band", None),
        P("comp", None, "band", "cores"),
        P(None, "cores"),
        P("comp", "cores"),
        P("cores", None),
        P(),
        P(),
    )
    out_specs = (P(None, "comp", "band", None), P("comp", None, "band", "cores"))
    return jax.shard_map(body, mesh=mesh, in_specs=in_specs, out_specs=out_specs, check_vma=False)
```
